32 devices in a mesh: rep: 8 (over y, x, core), exp: 4 (over z).
Axes of the slice: x: 2, y: 2, z: 4, core: 2. Of those that a mesh axis runs over, the one named last changes fastest.
Arguments:
- replay_buffer_rows: bfloat16 [4096, 3584], P(('rep', 'exp')), may hold values from -6 to 6
- shard_request_index: int32 [32, 8, 32], P(('rep', 'exp')), may hold values from 0 to 127
- replica_fetch_count: int32 [32, 8], P(('rep', 'exp')), may hold values from 0 to 32, as said below
- routes: int32 [4096, 1], P(('rep', 'exp')), may hold values from 0 to 3; in each aligned block of 128 rows (0 to 127, 128 to 255, ...) at most 56 rows name the same one
- router_route_weight: float32 [4096, 1], P(('rep', 'exp')), may hold values from 0.25 to 1
- output_gradient: bfloat16 [4096, 1024], P(('rep', 'exp')), may hold values from -0.119628906 to 0.119628906
- frozen_gate_weight: bfloat16 [4, 3584, 1024], P('exp'), may hold values from -0.09375 to 0.09375
- adapter_down_weight: bfloat16 [4, 3584, 128], P('exp'), may hold values from -0.09375 to 0.09375
- adapter_up_weight: bfloat16 [4, 128, 1024], P('exp'), may hold values from -0.5 to 0.5
Outputs:
- out_rows: bfloat16 [4096, 1024], P(('rep', 'exp'))
- down_adapter_gradient: float32 [4, 3584, 128], P('exp', 'rep')
- up_adapter_gradient: float32 [4, 128, 1024], P('exp', 'rep')
The draws below stay inside these ranges and needn't reach their ends.
Inputs may be any that keep to these rules, and one draw needn't show every extreme that they name: Each row replica_fetch_count[d, :] sums to 128, and every row has an entry equal to 32. `shard_request_index`: entry [s * 4 + c, r, j] is read only where j < replica_fetch_count[r * 4 + c, s]. `routes`: among the 128 rows of one device no expert is named more than 56 times, and that bound is reached.
All inputs are finite; a program needn't handle non-finite values.
Results may differ from the reference program's by a relative error of at most 0.0061.
Values may be sent and summed in bfloat16 or wider, within the bound.
No kernel may reach another device: no remote copies, remote signals or barrier semaphores. Data moves between devices by JAX's collectives and lax.ppermute only.
A program may use at most 64 MiB of HBM per device.

```python
import math
import jax
import jax.numpy as jnp
import numpy as np
from jax import lax

MODEL_DIM = 3584
HIDDEN_WIDTH = 1024
ADAPTER_RANK = 128
TOPK = 1
TOK_DEV = 128
BUF_DEV = 128
EXPERT_TOTAL = 4
TOKENS = 4096
BUF = 4096
FCAP = 32
CAP = 56
N_REP = 8
N_EXP = 4
DEVICES = 32


def draw_replica_fetch_count(key, part):
    mean_count = TOK_DEV // N_REP
    half_count = N_REP // 2
    row_count = N_REP * N_EXP
    order_keys = jax.random.split(jax.random.fold_in(key, 11), row_count)
    orders = jax.vmap(lambda single: jax.random.permutation(single, N_REP))(order_keys).astype(jnp.int32)
    moves = jax.random.randint(jax.random.fold_in(key, 12), (row_count, half_count), 0, mean_count + 1).astype(jnp.int32)
    moves = moves.at[:, 0].set(mean_count)
    values = jnp.concatenate([mean_count + moves, mean_count - moves], axis=1).astype(jnp.int32)
    row_index = jnp.broadcast_to(jnp.arange(row_count, dtype=jnp.int32)[:, None], (row_count, N_REP))
    counts = jnp.zeros((row_count, N_REP), jnp.int32).at[row_index, orders].set(values)
    return counts


def place_ends(entries, rng, smallest, top_value):
    longest = entries.shape.index(max(entries.shape))
    spots = []
    for shift in (0, 1):
        where = [jax.random.randint(jax.random.fold_in(rng, axis), (), 0, length) for axis, length in enumerate(entries.shape)]
        where[longest] = (where[longest] + shift) % entries.shape[longest]
        spots.append(tuple(where))
    return entries.at[spots[0]].set(smallest).at[spots[1]].set(top_value)


def level_of(rng, shape, pieces, least, top_value):
    def one(position, shards_of):
        steps = jax.random.uniform(jax.random.fold_in(jax.random.fold_in(rng, 6), position), (shards_of,), jnp.float32, least / len(pieces), top_value / len(pieces))
        return jnp.repeat(jnp.exp(steps), shape[position] // shards_of).reshape((-1,) + (1,) * (len(shape) - position - 1))

    level = one(*pieces[0])
    for cut in pieces[1:]:
        level = level * one(*cut)
    return level


def routed_block(rng, own, number, rows, count, top, reach, skew):
    order = jax.random.permutation(rng, count)
    packed, usual = shares(count, rows * top, reach, skew, True), shares(count, rows * top, reach, skew, False)
    places = jnp.arange(count)

    def named(sizes, turn):
        used = int((sizes > 0).sum())
        fixed = max(1, used // 4)
        passed = fixed + (places - fixed + turn * (used - fixed)) % max(1, count - fixed)
        return jnp.zeros((count,), jnp.int32).at[order[jnp.where(places < fixed, places, passed)]].set(jnp.asarray(sizes, jnp.int32))

    sizes = jnp.where(number % 4 == 0, named(packed, number // 4), named(usual, number - number // 4 - 1))
    mixed = jax.random.permutation(jax.random.fold_in(own, 3), count)
    donor, receiver = mixed[0:count // 2 * 2:2], mixed[1:count // 2 * 2:2]
    margin = jnp.minimum(sizes[donor] - 1, reach - sizes[receiver]) // 2
    margin = jnp.where((donor == order[0]) | (receiver == order[0]) | (sizes[receiver] == 0), 0, jnp.maximum(margin, 0))
    passed = jax.random.randint(jax.random.fold_in(own, 4), (count // 2,), 0, 1 << 20) % (margin + 1)
    sizes = sizes.at[donor].add(-passed).at[receiver].add(passed)
    items = jnp.searchsorted(jnp.cumsum(sizes), jnp.arange(rows * top), side="right").astype(jnp.int32)
    listing = items.reshape(top, rows).T
    listing = listing[jax.random.permutation(jax.random.fold_in(own, 1), rows)]
    turn = jax.random.randint(jax.random.fold_in(own, 2), (rows, 1), 0, top)
    return jnp.take_along_axis(listing, (jnp.arange(top)[None, :] + turn) % top, axis=1)


def shares(number_of, total, most, slope, full):
    portions = [(1 << 20) // math.isqrt(standing ** slope) + 1 for standing in range(1, number_of + 1)]
    largest = most if full else min(most, max(-(-total // number_of), total * portions[0] // sum(portions)))
    least = 1 if total - largest >= number_of - 1 else 0
    given, rest = [largest] + [least] * (number_of - 1), total - largest - least * (number_of - 1)
    while rest > 0:
        free = [i for i in range(1, number_of) if given[i] < largest] or [i for i in range(1, number_of) if given[i] < most]
        mass, budget = sum([portions[i] for i in free]), rest
        for i in free:
            addition = min(most - given[i], max(1, budget * portions[i] // mass), rest)
            given[i] = given[i] + addition
            rest = rest - addition
    return np.array(given)


def noise(key, shape, width, reach, pieces=(), kind=jnp.bfloat16):
    result = width * jax.random.normal(key, shape, jnp.float32)
    if pieces:
        result = result * level_of(key, shape, pieces, -0.22, 0.18)
    return jnp.clip(result, -reach, reach).astype(kind)


def setup_inputs(seed: int = 0) -> dict:
    seeds = jax.random.split(jax.random.key(seed), 10)
    replay_buffer_rows = noise(seeds[0], (BUF, MODEL_DIM), 1.0, 6.0, ((0, 32),))
    shard_request_index = place_ends(jax.random.randint(seeds[1], (DEVICES, N_REP, FCAP), 0, BUF_DEV), jax.random.fold_in(seeds[1], 1), 0, BUF_DEV - 1).astype(jnp.int32)
    replica_fetch_count = draw_replica_fetch_count(jax.random.fold_in(seeds[9], 71), 0)
    routes_keys = jax.random.split(jax.random.fold_in(seeds[3], 1), TOKENS // TOK_DEV)
    routes_turns = jax.random.permutation(jax.random.fold_in(seeds[3], 3), TOKENS // TOK_DEV)
    routes = jax.vmap(lambda own, number: routed_block(jax.random.fold_in(seeds[3], 2), own, number, TOK_DEV, EXPERT_TOTAL, TOPK, CAP, 2))(routes_keys, routes_turns).reshape((TOKENS, TOPK))
    router_route_weight = jnp.clip(0.25 + 0.75 * jax.random.uniform(seeds[4], (TOKENS, TOPK), jnp.float32) ** level_of(seeds[4], (TOKENS, TOPK), ((0, 32),), -0.2, 0.2), 0.25, 1.0)
    output_gradient = noise(seeds[5], (TOKENS, HIDDEN_WIDTH), 0.02, 0.119628906, ((0, 32),))
    frozen_gate_weight = noise(seeds[6], (EXPERT_TOTAL, MODEL_DIM, HIDDEN_WIDTH), MODEL_DIM ** -0.5, 0.09375, ((0, 4),))
    adapter_down_weight = noise(seeds[7], (EXPERT_TOTAL, MODEL_DIM, ADAPTER_RANK), MODEL_DIM ** -0.5, 0.09375, ((0, 4),))
    adapter_up_weight = noise(seeds[8], (EXPERT_TOTAL, ADAPTER_RANK, HIDDEN_WIDTH), ADAPTER_RANK ** -0.5, 0.5, ((0, 4),))
    return dict(replay_buffer_rows=replay_buffer_rows, shard_request_index=shard_request_index, replica_fetch_count=replica_fetch_count, routes=routes, router_route_weight=router_route_weight, output_gradient=output_gradient, frozen_gate_weight=frozen_gate_weight, adapter_down_weight=adapter_down_weight, adapter_up_weight=adapter_up_weight)


def silu_slope(pre_act):
    gate_value = jax.nn.sigmoid(pre_act)
    return gate_value * (1.0 + pre_act * (1.0 - gate_value))


def reference(replay_buffer_rows, shard_request_index, replica_fetch_count, routes, router_route_weight, output_gradient, frozen_gate_weight, adapter_down_weight, adapter_up_weight):
    device_count = N_REP * N_EXP
    row_ends = jnp.cumsum(replica_fetch_count, axis=1).astype(jnp.int32)
    row_starts = (row_ends - replica_fetch_count).astype(jnp.int32)
    positions = jnp.arange(TOK_DEV, dtype=jnp.int32)
    source = jnp.sum((row_ends[:, None, :] <= positions[None, :, None]).astype(jnp.int32), axis=2).astype(jnp.int32)
    offset = (positions[None, :] - jnp.take_along_axis(row_starts, source, axis=1)).astype(jnp.int32)
    device_ids = jnp.arange(device_count, dtype=jnp.int32)
    replica = device_ids // N_EXP
    column = device_ids % N_EXP
    server = (source * N_EXP + column[:, None]).astype(jnp.int32)
    local_row = shard_request_index[server, replica[:, None], offset]
    global_row = (server * BUF_DEV + local_row).reshape(-1).astype(jnp.int32)
    tokens = jnp.take(replay_buffer_rows, global_row, axis=0)

    slot_count = TOKENS * TOPK
    block_routes = routes.reshape(device_count, TOK_DEV * TOPK)
    expert_ids = jnp.arange(EXPERT_TOTAL, dtype=jnp.int32)
    chosen = (block_routes[:, :, None] == expert_ids[None, None, :]).astype(jnp.int32)
    slot_rank = jnp.sum((jnp.cumsum(chosen, axis=1) - 1) * chosen, axis=2).astype(jnp.int32)
    slot_device = jnp.repeat(device_ids, TOK_DEV * TOPK)
    slot_replica = (slot_device // N_EXP).astype(jnp.int32)
    slot_column = (slot_device % N_EXP).astype(jnp.int32)
    flat_expert = routes.reshape(-1).astype(jnp.int32)
    tile_pos = (slot_column * CAP + slot_rank.reshape(-1)).astype(jnp.int32)
    lookup_table = jnp.full((EXPERT_TOTAL, N_REP, N_EXP * CAP), slot_count, jnp.int32)
    lookup_table = lookup_table.at[flat_expert, slot_replica, tile_pos].set(jnp.arange(slot_count, dtype=jnp.int32))

    token_pad = jnp.concatenate([tokens, jnp.zeros((1, MODEL_DIM), jnp.bfloat16)], axis=0)
    slot_grad = (router_route_weight.reshape(-1, 1) * jnp.repeat(output_gradient, TOPK, axis=0).astype(jnp.float32)).astype(jnp.bfloat16)
    grad_pad = jnp.concatenate([slot_grad, jnp.zeros((1, HIDDEN_WIDTH), jnp.bfloat16)], axis=0)
    tile_len = N_EXP * CAP

    def single_expert_step(inputs):
        slot_ids, weight, down_map, up_map = inputs
        flat_ids = slot_ids.reshape(-1)
        token_ids = jnp.where(flat_ids < slot_count, flat_ids // TOPK, TOKENS).astype(jnp.int32)
        rows_x = jnp.take(token_pad, token_ids, axis=0)
        adapted_hidden = jnp.dot(rows_x, down_map, preferred_element_type=jnp.float32).astype(jnp.bfloat16)
        pre_act = jnp.dot(rows_x, weight, preferred_element_type=jnp.float32) + jnp.dot(adapted_hidden, up_map, preferred_element_type=jnp.float32)
        activated = jax.nn.silu(pre_act).astype(jnp.bfloat16)
        grad_rows = jnp.take(grad_pad, flat_ids, axis=0)
        preact_gradient = (grad_rows.astype(jnp.float32) * silu_slope(pre_act)).astype(jnp.bfloat16)
        back_reduced = jnp.dot(preact_gradient, up_map.T, preferred_element_type=jnp.float32).astype(jnp.bfloat16)
        shaped_x = rows_x.reshape(N_REP, tile_len, MODEL_DIM).astype(jnp.float32)
        shaped_back = back_reduced.reshape(N_REP, tile_len, ADAPTER_RANK).astype(jnp.float32)
        down_parts = jnp.einsum("rmd,rmk->rdk", shaped_x, shaped_back, precision=lax.Precision.HIGHEST)
        shaped_adapted = adapted_hidden.reshape(N_REP, tile_len, ADAPTER_RANK).astype(jnp.float32)
        shaped_grad = preact_gradient.reshape(N_REP, tile_len, HIDDEN_WIDTH).astype(jnp.float32)
        up_parts = jnp.einsum("rmk,rmf->rkf", shaped_adapted, shaped_grad, precision=lax.Precision.HIGHEST)
        down_sum = jnp.sum(down_parts, axis=0)
        up_sum = jnp.sum(up_parts, axis=0)
        return activated, down_sum, up_sum

    activated_rows_full, down_adapter_gradient, up_adapter_gradient = lax.map(single_expert_step, (lookup_table, frozen_gate_weight, adapter_down_weight, adapter_up_weight))
    slot_values = jnp.zeros((slot_count + 1, HIDDEN_WIDTH), jnp.bfloat16).at[lookup_table.reshape(-1)].set(activated_rows_full.reshape(-1, HIDDEN_WIDTH))
    slot_values = slot_values[:slot_count].reshape(TOKENS, TOPK, HIDDEN_WIDTH).astype(jnp.float32)
    out_rows = jnp.sum(router_route_weight[:, :, None] * slot_values, axis=1).astype(jnp.bfloat16)
    return out_rows, down_adapter_gradient, up_adapter_gradient
```

```python
import jax
import jax.numpy as jnp
from jax import lax
from jax.sharding import PartitionSpec as P

CHUNKS = 2


def silu_slope(pre_act):
    gate_value = jax.nn.sigmoid(pre_act)
    return gate_value * (1.0 + pre_act * (1.0 - gate_value))


def swap(block, step, exp_count):
    if step == 0:
        return block
    return lax.ppermute(block, "exp", [(i, i ^ step) for i in range(exp_count)])


def body(
    replay_buffer_rows,
    shard_request_index,
    replica_fetch_count,
    routes,
    router_route_weight,
    output_gradient,
    frozen_gate_weight,
    adapter_down_weight,
    adapter_up_weight,
):
    rep_count = lax.axis_size("rep")
    exp_count = lax.axis_size("exp")
    column = lax.axis_index("exp")
    token_count = routes.shape[0]
    shard_rows, model_width = replay_buffer_rows.shape
    fetch_slots = shard_request_index.shape[2]
    hidden_units = frozen_gate_weight.shape[2]
    rank_width = adapter_down_weight.shape[2]
    capacity = 7 * token_count // (4 * exp_count)
    tile_rows = exp_count * capacity
    fetched_rows = rep_count * fetch_slots
    bf16 = jnp.bfloat16
    f32 = jnp.float32

    asked = shard_request_index.reshape(fetched_rows, 1)
    serve = (asked == lax.broadcasted_iota(jnp.int32, (fetched_rows, shard_rows), 1)).astype(bf16)
    chunk_width = model_width // CHUNKS
    arrived = []
    for chunk in range(CHUNKS):
        part = replay_buffer_rows[:, chunk * chunk_width : (chunk + 1) * chunk_width]
        served = jnp.dot(serve, part, preferred_element_type=f32).astype(bf16)
        arrived.append(
            lax.all_to_all(
                served.reshape(rep_count, fetch_slots, chunk_width),
                "rep",
                split_axis=0,
                concat_axis=0,
                tiled=True,
            ).reshape(fetched_rows, chunk_width)
        )

    counts = replica_fetch_count.reshape(1, rep_count)
    row_ends = jnp.cumsum(counts, axis=1)
    row_starts = row_ends - counts
    positions = lax.broadcasted_iota(jnp.int32, (token_count, rep_count), 0)
    passed = row_ends <= positions
    source = jnp.sum(passed.astype(jnp.int32), axis=1, keepdims=True)
    here = lax.broadcasted_iota(jnp.int32, (token_count, rep_count), 1) == source
    start = jnp.sum(jnp.where(here, row_starts, 0), axis=1, keepdims=True)
    place = source * fetch_slots + positions[:, :1] - start
    block = jnp.bitwise_xor(routes, column)
    chosen = (block == lax.broadcasted_iota(jnp.int32, (token_count, exp_count), 1)).astype(jnp.int32)
    rank = jnp.sum((jnp.cumsum(chosen, axis=0) - 1) * chosen, axis=1, keepdims=True)
    target = block * capacity + rank
    slot_of = target == lax.broadcasted_iota(jnp.int32, (token_count, tile_rows), 1)
    home = slot_of.astype(bf16)
    place_of = (place == lax.broadcasted_iota(jnp.int32, (token_count, fetched_rows), 1)).astype(bf16)
    pick_rows = lax.dot_general(
        home, place_of, (((0,), (0,)), ((), ())), preferred_element_type=f32
    ).astype(bf16)

    scaled = (router_route_weight * output_gradient.astype(f32)).astype(bf16)
    grad_blocks = []
    for step in range(exp_count):
        lanes = slice(step * capacity, (step + 1) * capacity)
        sent = lax.dot_general(
            home[:, lanes], scaled, (((0,), (0,)), ((), ())), preferred_element_type=f32
        ).astype(bf16)
        grad_blocks.append(swap(sent, step, exp_count))
    grad_tile = jnp.concatenate(grad_blocks, axis=0)

    pre_act = jnp.zeros((tile_rows, hidden_units), f32)
    adapted = jnp.zeros((tile_rows, rank_width), f32)
    tiles = []
    for chunk in range(CHUNKS):
        blocks = []
        for step in range(exp_count):
            lanes = slice(step * capacity, (step + 1) * capacity)
            sent = jnp.dot(pick_rows[lanes], arrived[chunk], preferred_element_type=f32).astype(bf16)
            blocks.append(swap(sent, step, exp_count))
        tile = jnp.concatenate(blocks, axis=0)
        tiles.append(tile)
        part = slice(chunk * chunk_width, (chunk + 1) * chunk_width)
        adapted = adapted + jnp.dot(tile, adapter_down_weight[0, part], preferred_element_type=f32)
        pre_act = pre_act + jnp.dot(tile, frozen_gate_weight[0, part], preferred_element_type=f32)
    adapted = adapted.astype(bf16)
    pre_act = pre_act + jnp.dot(adapted, adapter_up_weight[0], preferred_element_type=f32)
    activated = jax.nn.silu(pre_act).astype(bf16)

    results = [
        swap(activated[step * capacity : (step + 1) * capacity], step, exp_count)
        for step in range(exp_count)
    ]
    picked = jnp.dot(home, jnp.concatenate(results, axis=0), preferred_element_type=f32)
    out_rows = (router_route_weight * picked).astype(bf16)

    preact_gradient = (grad_tile.astype(f32) * silu_slope(pre_act)).astype(bf16)
    up_term = lax.dot_general(
        adapted, preact_gradient, (((0,), (0,)), ((), ())), preferred_element_type=f32
    )
    back_reduced = lax.dot_general(
        preact_gradient, adapter_up_weight[0], (((1,), (1,)), ((), ())), preferred_element_type=f32
    ).astype(bf16)
    down_terms = [
        lax.dot_general(tile, back_reduced, (((0,), (0,)), ((), ())), preferred_element_type=f32)
        for tile in tiles
    ]
    down_term = jnp.concatenate(down_terms, axis=0).astype(bf16)
    down_sent = down_term.reshape(rep_count, model_width // rep_count, rank_width)
    up_rows = rank_width // rep_count
    up_lanes = hidden_units // rank_width
    up_sent = (
        up_term.astype(bf16)
        .reshape(rep_count, up_rows, up_lanes, rank_width)
        .transpose(0, 2, 1, 3)
        .reshape(rep_count, up_rows * up_lanes, rank_width)
    )
    terms = lax.all_to_all(
        jnp.concatenate([down_sent, up_sent], axis=1), "rep", split_axis=0, concat_axis=0, tiled=True
    )
    total = jnp.sum(terms.astype(f32), axis=0)
    down_grad = total[: model_width // rep_count]
    up_grad = (
        total[model_width // rep_count :]
        .reshape(up_lanes, up_rows, rank_width)
        .transpose(1, 0, 2)
        .reshape(up_rows, hidden_units)
    )
    return (out_rows, down_grad[None], up_grad[None])


def solution(mesh):
    placed = (
        P(("rep", "exp"), None),
        P(("rep", "exp"), None, None),
        P(("rep", "exp"), None),
        P(("rep", "exp"), None),
        P(("rep", "exp"), None),
        P(("rep", "exp"), None),
        P("exp", None, None),
        P("exp", None, None),
        P("exp", None, None),
    )
    return jax.shard_map(
        body,
        mesh=mesh,
        in_specs=placed,
        out_specs=(P(("rep", "exp"), None), P("exp", "rep", None), P("exp", "rep", None)),
        check_vma=False,
    )
```

```python
import functools

import jax
import jax.numpy as jnp
from jax import lax
from jax.experimental import pallas as pl
from jax.experimental.pallas import tpu as pltpu
from jax.sharding import PartitionSpec as P

CHUNKS = 2
VMEM_BYTES = 48 * 1024 * 1024
bf16 = jnp.bfloat16
f32 = jnp.float32
i32 = jnp.int32


def dot(a, b, contract=((1,), (0,))):
    return lax.dot_general(a, b, (contract, ((), ())), preferred_element_type=f32)


def call(kernel, out_shape, in_specs, scratch=(), flops=0, transcendentals=0, moved=0, name=None):
    return pl.pallas_call(
        kernel,
        out_shape=out_shape,
        grid=(1,),
        in_specs=in_specs,
        out_specs=jax.tree.map(whole, out_shape),
        scratch_shapes=list(scratch),
        cost_estimate=pl.CostEstimate(flops=flops, bytes_accessed=moved, transcendentals=transcendentals),
        compiler_params=pltpu.CompilerParams(vmem_limit_bytes=VMEM_BYTES),
        name=name,
    )


def whole(array):
    zeros = (0,) * len(array.shape)
    return pl.BlockSpec(array.shape, lambda i: zeros)


def smem(array):
    zeros = (0,) * len(array.shape)
    return pl.BlockSpec(array.shape, lambda i: zeros, memory_space=pltpu.SMEM)


def shape(dims, kind):
    return jax.ShapeDtypeStruct(dims, kind)


def swap_exp(block, step, exp_count):
    if step == 0:
        return block
    return lax.ppermute(block, "exp", [(i, i ^ step) for i in range(exp_count)])


def swap_rep(block, step, rep_count):
    if step == 0:
        return block
    return lax.ppermute(block, "rep", [(i, i ^ step) for i in range(rep_count)])


def prepare_kernel(fetch_slots, capacity, padded, counts, routes, weight, grads, pick, home, *sent):
    tokens = routes.shape[0]
    rep_count = counts.shape[1]
    exp_count = len(sent)
    replica = lax.axis_index("rep")
    column = lax.axis_index("exp")
    position = lax.broadcasted_iota(i32, (tokens, 1), 0)
    source = jnp.zeros((tokens, 1), i32)
    start = jnp.zeros((tokens, 1), i32)
    end = jnp.int32(0)
    for shard in range(rep_count):
        end = end + counts[0, shard]
        passed = position >= end
        source = source + passed.astype(i32)
        start = jnp.where(passed, end, start)
    place = jnp.bitwise_xor(source, replica) * fetch_slots + position - start
    place_of = place == lax.broadcasted_iota(i32, (tokens, rep_count * fetch_slots), 1)

    block = jnp.bitwise_xor(routes[...], column)
    chosen = block == lax.broadcasted_iota(i32, (tokens, exp_count), 1)
    above = lax.broadcasted_iota(i32, (tokens, tokens), 1) < lax.broadcasted_iota(i32, (tokens, tokens), 0)
    ranks = dot(above.astype(f32).astype(bf16), chosen.astype(f32).astype(bf16))
    rank = jnp.sum(jnp.where(chosen, ranks, 0.0), axis=1, keepdims=True).astype(i32)
    target = block * padded + rank
    slots = exp_count * padded
    home_of = (target == lax.broadcasted_iota(i32, (tokens, slots), 1)).astype(f32).astype(bf16)
    home[...] = home_of
    pick[...] = dot(home_of, place_of.astype(f32).astype(bf16), ((0,), (0,))).astype(bf16)
    scaled = (weight[...] * grads[...].astype(f32)).astype(bf16)
    by_slot = dot(home_of, scaled, ((0,), (0,))).astype(bf16)
    for step in range(exp_count):
        sent[step][...] = by_slot[step * padded : step * padded + capacity]


def serve_kernel(own_rows, pair_rows, own_table, pair_table, *sent):
    rep_count, fetch_slots = own_table.shape[1:]
    shard_rows = own_rows.shape[0]
    replica = lax.axis_index("rep")
    asked = []
    for step in range(0, rep_count, 2):
        wanted = jnp.bitwise_xor(replica, step)
        asked.append(own_table[0, pl.ds(wanted, 1), :])
        asked.append(pair_table[0, pl.ds(wanted, 1), :] + shard_rows)
    asked = jnp.concatenate(asked, axis=1)
    serve = (asked == lax.broadcasted_iota(i32, (2 * shard_rows, rep_count * fetch_slots), 0)).astype(f32).astype(bf16)
    rows = jnp.concatenate([own_rows[...], pair_rows[...]], axis=0)
    served = dot(serve, rows, ((0,), (0,))).astype(bf16)
    for number, block in enumerate(sent):
        block[...] = served[number * 2 * fetch_slots : (number + 1) * 2 * fetch_slots]


def pick_kernel(capacity, padded, sources, pick, *refs):
    arrived, sent = refs[:sources], refs[sources:]
    rows = jnp.concatenate([block[...] for block in arrived], axis=0)
    by_slot = dot(pick[...], rows).astype(bf16)
    for step in range(len(sent)):
        sent[step][...] = by_slot[step * padded : step * padded + capacity]


def fill(tile, blocks, capacity, padded):
    tile[...] = jnp.zeros(tile.shape, tile.dtype)
    for step, block in enumerate(blocks):
        tile[step * padded : step * padded + capacity, :] = block[...]


def partial_kernel(capacity, padded, gate, down, *refs):
    blocks = refs[:-3]
    tile, pre_act, adapted = refs[-3:]
    fill(tile, blocks, capacity, padded)
    pre_act[...] = dot(tile[...], gate[0])
    adapted[...] = dot(tile[...], down[0])


def finish_kernel(
    capacity, padded, exp_count, first, pre_first, adapted_first, gate, down, up, *refs
):
    blocks, refs = refs[:exp_count], refs[exp_count:]
    grads, refs = refs[:exp_count], refs[exp_count:]
    activated, refs = refs[:exp_count], refs[exp_count:]
    keep, give, tile, grad_tile, down_term, up_term = refs
    fill(tile, blocks, capacity, padded)
    fill(grad_tile, grads, capacity, padded)
    adapted = (adapted_first[...] + dot(tile[...], down[0])).astype(bf16)
    pre_act = pre_first[...] + dot(tile[...], gate[0]) + dot(adapted, up[0])
    gate_value = jax.nn.sigmoid(pre_act)
    rows = (pre_act * gate_value).astype(bf16)
    for step in range(exp_count):
        activated[step][...] = rows[step * padded : step * padded + capacity]
    slope = gate_value * (1.0 + pre_act * (1.0 - gate_value))
    grad_pre = (grad_tile[...].astype(f32) * slope).astype(bf16)
    back = dot(grad_pre, up[0], ((1,), (1,))).astype(bf16)
    pairs = keep.shape[0]
    down_rows = down_term.shape[1]
    up_rows, hidden_units = up_term.shape[1:]
    lanes = keep.shape[2]
    by_owner = first.shape[1] // down_rows
    for half, rows in enumerate((first, tile)):
        part = dot(rows[...], back, ((0,), (0,))).astype(bf16)
        for number in range(by_owner):
            down_term[half * by_owner + number] = part[number * down_rows : (number + 1) * down_rows]
    part = dot(adapted, grad_pre, ((0,), (0,)))
    for number in range(2 * pairs):
        up_term[number] = part[number * up_rows : (number + 1) * up_rows].astype(bf16)

    replica = lax.axis_index("rep")
    for number in range(pairs):
        for flip, target in ((0, keep), (1, give)):
            owner = jnp.bitwise_xor(replica, 2 * number + flip)
            target[number, :down_rows] = down_term[owner]
            mine = up_term[owner]
            for part in range(hidden_units // lanes):
                base = down_rows + part * up_rows
                target[number, base : base + up_rows] = mine[:, part * lanes : (part + 1) * lanes]


def combine_kernel(capacity, padded, home, weight, *refs):
    blocks = refs[:-2]
    out, tile = refs[-2:]
    fill(tile, blocks, capacity, padded)
    out[...] = (weight[...] * dot(home[...], tile[...])).astype(bf16)


def total_kernel(*refs):
    terms, (down_grad, up_grad) = refs[:-2], refs[-2:]
    total = terms[0][...].astype(f32)
    for term in terms[1:]:
        total = total + term[...].astype(f32)
    down_rows = down_grad.shape[1]
    up_rows, hidden_units = up_grad.shape[1:]
    lanes = total.shape[1]
    down_grad[0] = total[:down_rows]
    for part in range(hidden_units // lanes):
        base = down_rows + part * up_rows
        up_grad[0, :, part * lanes : (part + 1) * lanes] = total[base : base + up_rows]


def body(
    replay_buffer_rows,
    shard_request_index,
    replica_fetch_count,
    routes,
    router_route_weight,
    output_gradient,
    frozen_gate_weight,
    adapter_down_weight,
    adapter_up_weight,
):
    rep_count = lax.axis_size("rep")
    exp_count = lax.axis_size("exp")
    pairs = rep_count // 2
    token_count = routes.shape[0]
    shard_rows, model_width = replay_buffer_rows.shape
    fetch_slots = shard_request_index.shape[2]
    hidden_units = frozen_gate_weight.shape[2]
    rank_width = adapter_down_weight.shape[2]
    capacity = 7 * token_count // (4 * exp_count)
    padded = -(-capacity // 16) * 16
    slots = exp_count * padded
    fetched_rows = rep_count * fetch_slots
    chunk_width = model_width // CHUNKS

    pair_table = swap_rep(shard_request_index, 1, rep_count)
    pair_rows = swap_rep(replay_buffer_rows, 1, rep_count)

    prepared = call(
        functools.partial(prepare_kernel, fetch_slots, capacity, padded),
        [shape((slots, fetched_rows), bf16), shape((token_count, slots), bf16)]
        + [shape((capacity, hidden_units), bf16)] * exp_count,
        [smem(replica_fetch_count), whole(routes), whole(router_route_weight), whole(output_gradient)],
        flops=2 * token_count * slots * (hidden_units + fetched_rows),
        name="prepare",
    )(replica_fetch_count, routes, router_route_weight, output_gradient)
    pick, home, grads = prepared[0], prepared[1], prepared[2:]

    def columns(rows, chunk):
        return pl.BlockSpec((rows, chunk_width), lambda i: (0, chunk))

    def weight_rows(array, chunk):
        return pl.BlockSpec((1, chunk_width, array.shape[2]), lambda i: (0, chunk, 0))

    arrived = []
    for chunk in range(CHUNKS):
        served = call(
            serve_kernel,
            [shape((2 * fetch_slots, chunk_width), bf16)] * pairs,
            [columns(shard_rows, chunk)] * 2 + [whole(shard_request_index)] * 2,
            flops=4 * fetched_rows * shard_rows * chunk_width,
            name="serve",
        )(replay_buffer_rows, pair_rows, shard_request_index, pair_table)
        arrived.append([swap_rep(block, 2 * number, rep_count) for number, block in enumerate(served)])

    grads = [swap_exp(block, step, exp_count) for step, block in enumerate(grads)]

    blocks = []
    for chunk in range(CHUNKS):
        sent = call(
            functools.partial(pick_kernel, capacity, padded, pairs),
            [shape((capacity, chunk_width), bf16)] * exp_count,
            [whole(pick)] + [whole(block) for block in arrived[chunk]],
            flops=2 * slots * fetched_rows * chunk_width,
            name="pick",
        )(pick, *arrived[chunk])
        blocks.append([swap_exp(block, step, exp_count) for step, block in enumerate(sent)])

    first, pre_first, adapted_first = call(
        functools.partial(partial_kernel, capacity, padded),
        [shape((slots, chunk_width), bf16), shape((slots, hidden_units), f32), shape((slots, rank_width), f32)],
        [weight_rows(frozen_gate_weight, 0), weight_rows(adapter_down_weight, 0)]
        + [whole(block) for block in blocks[0]],
        flops=2 * slots * chunk_width * (hidden_units + rank_width),
        name="partial",
    )(frozen_gate_weight, adapter_down_weight, *blocks[0])

    term_rows = (model_width + rank_width * hidden_units // rank_width) // rep_count
    finished = call(
        functools.partial(finish_kernel, capacity, padded, exp_count),
        [shape((capacity, hidden_units), bf16)] * exp_count + [shape((pairs, term_rows, rank_width), bf16)] * 2,
        [whole(first), whole(pre_first), whole(adapted_first)]
        + [weight_rows(frozen_gate_weight, 1), weight_rows(adapter_down_weight, 1), whole(adapter_up_weight)]
        + [whole(block) for block in blocks[1]]
        + [whole(block) for block in grads],
        scratch=[
            pltpu.VMEM((slots, chunk_width), bf16),
            pltpu.VMEM((slots, hidden_units), bf16),
            pltpu.VMEM((rep_count, model_width // rep_count, rank_width), bf16),
            pltpu.VMEM((rep_count, rank_width // rep_count, hidden_units), bf16),
        ],
        flops=4 * slots * chunk_width * (hidden_units + rank_width),
        name="finish",
    )(
        first,
        pre_first,
        adapted_first,
        frozen_gate_weight,
        adapter_down_weight,
        adapter_up_weight,
        *blocks[1],
        *grads,
    )
    activated, (keep, give) = finished[:exp_count], finished[exp_count:]

    pair_terms = swap_rep(give, 1, rep_count)
    results = [swap_exp(block, step, exp_count) for step, block in enumerate(activated)]
    chip_terms = (keep.astype(f32) + pair_terms.astype(f32)).astype(bf16)
    terms = [swap_rep(chip_terms[number], 2 * number, rep_count) for number in range(pairs)]

    out_rows = call(
        functools.partial(combine_kernel, capacity, padded),
        shape((token_count, hidden_units), bf16),
        [whole(home), whole(router_route_weight)] + [whole(block) for block in results],
        scratch=[pltpu.VMEM((slots, hidden_units), bf16)],
        flops=2 * token_count * slots * hidden_units,
        name="combine",
    )(home, router_route_weight, *results)

    down_grad, up_grad = call(
        total_kernel,
        [
            shape((1, model_width // rep_count, rank_width), f32),
            shape((1, rank_width // rep_count, hidden_units), f32),
        ],
        [whole(term) for term in terms],
        name="total",
    )(*terms)
    return (out_rows, down_grad, up_grad)


def solution(mesh):
    placed = (
        P(("rep", "exp"), None),
        P(("rep", "exp"), None, None),
        P(("rep", "exp"), None),
        P(("rep", "exp"), None),
        P(("rep", "exp"), None),
        P(("rep", "exp"), None),
        P("exp", None, None),
        P("exp", None, None),
        P("exp", None, None),
    )
    return jax.shard_map(
        body,
        mesh=mesh,
        in_specs=placed,
        out_specs=(P(("rep", "exp"), None), P("exp", "rep", None), P("exp", "rep", None)),
        check_vma=False,
    )
```

```python
import functools

import jax
import jax.numpy as jnp
from jax import lax
from jax.experimental import pallas as pl
from jax.experimental.pallas import tpu as pltpu
from jax.sharding import PartitionSpec as P

CHUNKS = 2
bf16 = jnp.bfloat16
f32 = jnp.float32
i32 = jnp.int32


def dot(a, b, contract=((1,), (0,))):
    return lax.dot_general(a, b, (contract, ((), ())), preferred_element_type=f32)


def call(kernel, out_shape, operands, counts=None, resident=(), far=(), stored=(), scratch=(), flops=0, vmem=16, name=None):
    first_out = len(operands)
    away = [number for number, array in enumerate(operands) if any(array is other for other in far)]
    moved = [*away, *(first_out + number for number in stored)]
    arrays = [*operands, *out_shape]

    def moving(*refs):
        inner = list(refs)
        copies = {}
        if moved:
            *inner, sems = inner
            near = inner[len(inner) - len(moved) :]
            inner = inner[: len(inner) - len(moved)]
            for place, number in enumerate(moved):
                ends = (inner[number], near[place]) if number < first_out else (near[place], inner[number])
                copies[number] = pltpu.make_async_copy(*ends, sems.at[place])
                inner[number] = near[place]
        for number in away:
            copies[number].start()
        for number in away:
            copies[number].wait()
        kernel(*inner)
        for number in moved[len(away) :]:
            copies[number].start()
        for number in moved[len(away) :]:
            copies[number].wait()

    def space(number):
        array = arrays[number]
        zeros = (0,) * len(array.shape)
        if number in moved:
            return pl.BlockSpec(memory_space=pltpu.HBM)
        if any(array is other for other in resident):
            return pl.BlockSpec(memory_space=pltpu.VMEM)
        if array is counts:
            return pl.BlockSpec(memory_space=pltpu.SMEM)
        return pl.BlockSpec(array.shape, lambda i: zeros)

    near = [pltpu.VMEM(arrays[number].shape, arrays[number].dtype) for number in moved]
    operands = [
        pltpu.with_memory_space_constraint(array, pltpu.HBM) if number in away else array
        for number, array in enumerate(operands)
    ]
    return pl.pallas_call(
        moving,
        out_shape=[
            pltpu.HBM(out.shape, out.dtype) if number in stored else out for number, out in enumerate(out_shape)
        ],
        grid=(1,),
        in_specs=[space(number) for number in range(first_out)],
        out_specs=[space(first_out + number) for number in range(len(out_shape))],
        scratch_shapes=[*scratch, *near] + ([pltpu.SemaphoreType.DMA((len(moved),))] if moved else []),
        cost_estimate=pl.CostEstimate(flops=flops, bytes_accessed=flops // 300, transcendentals=0),
        compiler_params=pltpu.CompilerParams(vmem_limit_bytes=vmem * 1024 * 1024),
        name=name,
    )(*operands)


def shape(dims, kind):
    return jax.ShapeDtypeStruct(dims, kind)


def swap_exp(block, step, exp_count):
    if step == 0:
        return block
    return lax.ppermute(block, "exp", [(i, i ^ step) for i in range(exp_count)])


def swap_core(block, rep_count):
    return lax.ppermute(block, "rep", [(i, i ^ 1) for i in range(rep_count)])


def swap_chip(block, step, rep_count):
    if step == 0:
        return block
    return lax.ppermute(block, "rep", [(i, i ^ (2 * step)) for i in range(rep_count)])


def between_chips(blocks, rep_count):
    cores = [list(range(core, rep_count, 2)) for core in range(2)]
    return lax.all_to_all(blocks, "rep", 0, 0, axis_index_groups=cores, tiled=True)


def upright(row):
    count = row.shape[1]
    same = lax.broadcasted_iota(i32, (count, count), 0) == lax.broadcasted_iota(i32, (count, count), 1)
    return jnp.sum(jnp.where(same, row, jnp.zeros_like(row)), axis=1, keepdims=True)


def one_hot(spots):
    return spots.astype(f32).astype(bf16)


def slot_spots(capacity, padded, exp_count, routes):
    tokens = routes.shape[1]
    block = jnp.bitwise_xor(upright(routes[...]), lax.axis_index("exp"))
    chosen = block == lax.broadcasted_iota(i32, (tokens, exp_count), 1)
    above = lax.broadcasted_iota(i32, (tokens, tokens), 1) < lax.broadcasted_iota(i32, (tokens, tokens), 0)
    ranks = dot(one_hot(above), one_hot(chosen))
    rank = jnp.sum(jnp.where(chosen, ranks, 0.0), axis=1, keepdims=True).astype(i32)
    target = block * padded + rank
    return one_hot(target == lax.broadcasted_iota(i32, (tokens, exp_count * padded), 1))


def prepare_kernel(fetch_slots, capacity, padded, exp_count, counts, routes, pick, pick_swapped, home):
    tokens = routes.shape[1]
    rep_count = counts.shape[1]
    replica = lax.axis_index("rep")
    position = lax.broadcasted_iota(i32, (tokens, 1), 0)
    source = jnp.zeros((tokens, 1), i32)
    start = jnp.zeros((tokens, 1), i32)
    end = jnp.int32(0)
    for shard in range(rep_count):
        end = end + counts[0, shard]
        passed = position >= end
        source = source + passed.astype(i32)
        start = jnp.where(passed, end, start)
    home_of = slot_spots(capacity, padded, exp_count, routes)
    home[...] = home_of

    places = lax.broadcasted_iota(i32, (tokens, rep_count * fetch_slots), 1)
    other = jnp.bitwise_and(jnp.bitwise_xor(source, replica), 1)
    even = source - jnp.bitwise_and(source, 1)
    apart = jnp.bitwise_xor(even, replica - jnp.bitwise_and(replica, 1))
    for chip, matrix in ((even, pick), (apart, pick_swapped)):
        place = (chip + other) * fetch_slots + position - start
        matrix[...] = dot(home_of, one_hot(place == places), ((0,), (0,))).astype(bf16)


def part_of(chunk, width):
    return slice(chunk * width, (chunk + 1) * width)


def serve(table, rows, first):
    rep_count, fetch_slots = table.shape[1:]
    core = jnp.bitwise_and(lax.axis_index("rep"), 1)
    asked = [table[0, pl.ds(jnp.bitwise_xor(2 * chip, first) + core, 1), :] for chip in range(rep_count // 2)]
    asked = jnp.concatenate(asked, axis=1)
    chosen = asked == lax.broadcasted_iota(i32, (rows.shape[0], asked.shape[1]), 0)
    found = dot(one_hot(chosen), rows, ((0,), (0,))).astype(bf16)
    return [found[chip * fetch_slots : (chip + 1) * fetch_slots] for chip in range(rep_count // 2)]


def begin_kernel(capacity, padded, table, rows, routes, weight, grads, served, *sent):
    for chip, found in enumerate(serve(table, rows[:, : served.shape[2]], 0)):
        served[chip] = found
    home = slot_spots(capacity, padded, len(sent), routes)
    scaled = (upright(weight[...]) * grads[...].astype(f32)).astype(bf16)
    by_slot = dot(home, scaled, ((0,), (0,))).astype(bf16)
    for step in range(len(sent)):
        sent[step][...] = by_slot[step * padded : step * padded + capacity]


def serve_first_kernel(table, rows, own, served):
    fetch_slots = own.shape[1]
    for chip, found in enumerate(serve(table, rows[:, : served.shape[2]], 0)):
        served[chip, :fetch_slots] = own[chip]
        served[chip, fetch_slots:] = found


def serve_last_kernel(own_table, own_rows, pair_table, pair_rows, *served):
    fetch_slots = own_table.shape[2]
    part = part_of(1, served[0].shape[1])
    replica = lax.axis_index("rep")
    first = replica - jnp.bitwise_and(replica, 1)
    for block, found in zip(served, serve(own_table, own_rows[:, part], first)):
        block[:fetch_slots] = found
    for block, found in zip(served, serve(pair_table, pair_rows[:, part], first)):
        block[fetch_slots:] = found


def pick_first_kernel(capacity, padded, pick, arrived, *refs):
    *grads, sent, grad_tile = refs
    fill(grad_tile, grads, capacity, padded)
    chips, rows, width = arrived.shape
    by_slot = dot(pick[...], arrived[...].reshape(chips * rows, width)).astype(bf16)
    column = lax.axis_index("exp")
    for step in range(sent.shape[0]):
        sent[jnp.bitwise_xor(column, step)] = by_slot[step * padded : step * padded + capacity]


def pick_last_kernel(capacity, padded, chips, pick, *refs):
    arrived, sent = refs[:chips], refs[chips:]
    rows = jnp.concatenate([block[...] for block in arrived], axis=0)
    by_slot = dot(pick[...], rows).astype(bf16)
    for step in range(len(sent)):
        sent[step][...] = by_slot[step * padded : step * padded + capacity]


def fill(tile, blocks, capacity, padded):
    tile[...] = jnp.zeros(tile.shape, tile.dtype)
    for step, block in enumerate(blocks):
        tile[step * padded : step * padded + capacity, :] = block[...]


def partial_kernel(capacity, padded, gate, down, arrived, tile, pre_act, adapted):
    column = lax.axis_index("exp")
    tile[...] = jnp.zeros(tile.shape, tile.dtype)
    for step in range(arrived.shape[0]):
        tile[step * padded : step * padded + capacity, :] = arrived[jnp.bitwise_xor(column, step)]
    part = part_of(0, tile.shape[1])
    pre_act[...] = dot(tile[...], gate[0, part])
    adapted[...] = dot(tile[...], down[0, part])


def finish_kernel(
    capacity, padded, exp_count, grad_tile, first, pre_first, adapted_first, gate, down, up, *refs
):
    blocks, refs = refs[:exp_count], refs[exp_count:]
    activated, refs = refs[:exp_count], refs[exp_count:]
    keep, give, tile, down_term, up_term = refs
    fill(tile, blocks, capacity, padded)
    part = part_of(1, tile.shape[1])
    adapted = (adapted_first[...] + dot(tile[...], down[0, part])).astype(bf16)
    pre_act = pre_first[...] + dot(tile[...], gate[0, part]) + dot(adapted, up[0])
    gate_value = jax.nn.sigmoid(pre_act)
    rows = (pre_act * gate_value).astype(bf16)
    for step in range(exp_count):
        activated[step][...] = rows[step * padded : step * padded + capacity]
    slope = gate_value * (1.0 + pre_act * (1.0 - gate_value))
    grad_pre = (grad_tile[...].astype(f32) * slope).astype(bf16)
    back = dot(grad_pre, up[0], ((1,), (1,))).astype(bf16)
    pairs = keep.shape[0]
    down_rows = down_term.shape[1]
    up_rows, hidden_units = up_term.shape[1:]
    lanes = keep.shape[2]
    by_owner = first.shape[1] // down_rows
    for half, rows in enumerate((first, tile)):
        part = dot(rows[...], back, ((0,), (0,)))
        for number in range(by_owner):
            down_term[half * by_owner + number] = part[number * down_rows : (number + 1) * down_rows]
    part = dot(adapted, grad_pre, ((0,), (0,)))
    for number in range(2 * pairs):
        up_term[number] = part[number * up_rows : (number + 1) * up_rows]

    replica = lax.axis_index("rep")
    for chip in range(pairs):
        for flip, target in ((0, keep), (1, give)):
            owner = jnp.bitwise_xor(replica, 2 * chip + flip)
            target[chip, :down_rows] = down_term[owner].astype(target.dtype)
            mine = up_term[owner].astype(target.dtype)
            for part in range(hidden_units // lanes):
                base = down_rows + part * up_rows
                target[chip, base : base + up_rows] = mine[:, part * lanes : (part + 1) * lanes]


def combine_kernel(capacity, padded, home, weight, *refs):
    blocks = refs[:-2]
    out, tile = refs[-2:]
    fill(tile, blocks, capacity, padded)
    out[...] = (upright(weight[...]) * dot(home[...], tile[...])).astype(bf16)


def total_kernel(*refs):
    *terms, down_grad, up_grad = refs
    total = terms[0][...].astype(f32)
    for term in terms[1:]:
        total = total + term[...].astype(f32)
    down_rows = down_grad.shape[1]
    up_rows, hidden_units = up_grad.shape[1:]
    lanes = total.shape[1]
    down_grad[0] = total[:down_rows]
    for part in range(hidden_units // lanes):
        base = down_rows + part * up_rows
        up_grad[0, :, part * lanes : (part + 1) * lanes] = total[base : base + up_rows]


def body(
    replay_buffer_rows,
    shard_request_index,
    replica_fetch_count,
    routes,
    router_route_weight,
    output_gradient,
    frozen_gate_weight,
    adapter_down_weight,
    adapter_up_weight,
):
    rep_count = lax.axis_size("rep")
    exp_count = lax.axis_size("exp")
    pairs = rep_count // 2
    token_count = routes.shape[0]
    shard_rows, model_width = replay_buffer_rows.shape
    fetch_slots = shard_request_index.shape[2]
    hidden_units = frozen_gate_weight.shape[2]
    rank_width = adapter_down_weight.shape[2]
    capacity = 7 * token_count // (4 * exp_count)
    padded = -(-capacity // 16) * 16
    slots = exp_count * padded
    fetched_rows = rep_count * fetch_slots
    chunk_width = model_width // CHUNKS

    routes_row = routes.reshape(1, token_count)
    weight_row = router_route_weight.reshape(1, token_count)

    pair_rows = swap_core(replay_buffer_rows, rep_count)
    pair_table = swap_core(shard_request_index, rep_count)
    operands = [shard_request_index, replay_buffer_rows, routes_row, weight_row, output_gradient]
    own_served, *grads = call(
        functools.partial(begin_kernel, capacity, padded),
        [shape((pairs, fetch_slots, chunk_width), bf16)] + [shape((capacity, hidden_units), bf16)] * exp_count,
        operands,
        far=operands,
        flops=2 * token_count * slots * hidden_units,
        name="begin",
    )
    (served,) = call(
        serve_first_kernel,
        [shape((pairs, 2 * fetch_slots, chunk_width), bf16)],
        [pair_table, pair_rows, own_served],
        stored=[0],
        flops=2 * fetched_rows * shard_rows * chunk_width,
        name="serve_first",
    )
    served, *grads, routes_row = lax.optimization_barrier((served, *grads, routes_row))
    arrived = between_chips(served, rep_count)
    grads = [swap_exp(block, step, exp_count) for step, block in enumerate(grads)]
    pick, pick_swapped, home = call(
        functools.partial(prepare_kernel, fetch_slots, capacity, padded, exp_count),
        [shape((slots, fetched_rows), bf16)] * 2 + [shape((token_count, slots), bf16)],
        [replica_fetch_count, routes_row],
        counts=replica_fetch_count,
        stored=[0, 1, 2],
        flops=4 * token_count * slots * fetched_rows,
        name="prepare",
    )
    sent, grad_tile = call(
        functools.partial(pick_first_kernel, capacity, padded),
        [shape((exp_count, capacity, chunk_width), bf16), shape((slots, hidden_units), bf16)],
        [pick, arrived, *grads],
        far=[pick],
        stored=[0, 1],
        flops=2 * slots * fetched_rows * chunk_width,
        name="pick_first",
    )

    pair_rows, sent = lax.optimization_barrier((pair_rows, sent))
    first_blocks = lax.all_to_all(sent, "exp", 0, 0, tiled=True)
    served = call(
        serve_last_kernel,
        [shape((2 * fetch_slots, chunk_width), bf16)] * pairs,
        [shard_request_index, replay_buffer_rows, pair_table, pair_rows],
        far=[shard_request_index, pair_table],
        flops=2 * fetched_rows * shard_rows * chunk_width,
        name="serve_last",
    )
    arrived = [swap_chip(block, step, rep_count) for step, block in enumerate(served)]
    sent = call(
        functools.partial(pick_last_kernel, capacity, padded, pairs),
        [shape((capacity, chunk_width), bf16)] * exp_count,
        [pick_swapped, *arrived],
        flops=2 * slots * fetched_rows * chunk_width,
        name="pick_last",
    )
    last_blocks = [swap_exp(block, step, exp_count) for step, block in enumerate(sent)]

    first, pre_first, adapted_first = call(
        functools.partial(partial_kernel, capacity, padded),
        [shape((slots, chunk_width), bf16), shape((slots, hidden_units), f32), shape((slots, rank_width), f32)],
        [frozen_gate_weight, adapter_down_weight, first_blocks],
        resident=[frozen_gate_weight, adapter_down_weight],
        flops=2 * slots * chunk_width * (hidden_units + rank_width),
        name="partial",
    )

    term_rows = (model_width + rank_width * hidden_units // rank_width) // rep_count
    *activated, keep, give = call(
        functools.partial(finish_kernel, capacity, padded, exp_count),
        [shape((capacity, hidden_units), bf16)] * exp_count + [shape((pairs, term_rows, rank_width), kind) for kind in (f32, bf16)],
        [
            grad_tile,
            first,
            pre_first,
            adapted_first,
            frozen_gate_weight,
            adapter_down_weight,
            adapter_up_weight,
            *last_blocks,
        ],
        resident=[frozen_gate_weight, adapter_down_weight],
        scratch=[
            pltpu.VMEM((slots, chunk_width), bf16),
            pltpu.VMEM((rep_count, model_width // rep_count, rank_width), f32),
            pltpu.VMEM((rep_count, rank_width // rep_count, hidden_units), f32),
        ],
        flops=4 * slots * chunk_width * (hidden_units + rank_width),
        name="finish",
    )

    pair_terms = swap_core(give, rep_count)
    results = [swap_exp(block, step, exp_count) for step, block in enumerate(activated)]
    terms = keep + pair_terms.astype(f32)
    while terms.shape[0] > 2:
        half = terms.shape[0] // 2
        terms = terms[:half] + swap_chip(terms[half:].astype(bf16), half, rep_count).astype(f32)
    last_terms = [terms[0], swap_chip(terms[1].astype(bf16), 1, rep_count)]

    down_grad, up_grad = call(
        total_kernel,
        [
            shape((1, model_width // rep_count, rank_width), f32),
            shape((1, rank_width // rep_count, hidden_units), f32),
        ],
        last_terms,
        name="total",
    )
    down_grad, *results = lax.optimization_barrier((down_grad, *results))
    (out_rows,) = call(
        functools.partial(combine_kernel, capacity, padded),
        [shape((token_count, hidden_units), bf16)],
        [home, weight_row, *results],
        scratch=[pltpu.VMEM((slots, hidden_units), bf16)],
        flops=2 * token_count * slots * hidden_units,
        name="combine",
    )
    return (out_rows, down_grad, up_grad)


def solution(mesh):
    placed = (
        P(("rep", "exp"), None),
        P(("rep", "exp"), None, None),
        P(("rep", "exp"), None),
        P(("rep", "exp"), None),
        P(("rep", "exp"), None),
        P(("rep", "exp"), None),
        P("exp", None, None),
        P("exp", None, None),
        P("exp", None, None),
    )
    return jax.shard_map(
        body,
        mesh=mesh,
        in_specs=placed,
        out_specs=(P(("rep", "exp"), None), P("exp", "rep", None), P("exp", "rep", None)),
        check_vma=False,
    )
```

```python
import functools

import jax
import jax.numpy as jnp
from jax import lax
from jax.experimental import pallas as pl
from jax.experimental.pallas import tpu as pltpu
from jax.sharding import PartitionSpec as P

FIRST_PART = 1
PARTS = 2
bf16 = jnp.bfloat16
f32 = jnp.float32
i32 = jnp.int32


def dot(a, b, contract=((1,), (0,))):
    return lax.dot_general(a, b, (contract, ((), ())), preferred_element_type=f32)


def call(kernel, out_shape, operands, counts=None, resident=(), far=(), stored=(), scratch=(), flops=0, vmem=16, name=None):
    first_out = len(operands)
    away = [number for number, array in enumerate(operands) if any(array is other for other in far)]
    moved = [*away, *(first_out + number for number in stored)]
    arrays = [*operands, *out_shape]

    def moving(*refs):
        inner = list(refs)
        copies = {}
        if moved:
            *inner, sems = inner
            near = inner[len(inner) - len(moved) :]
            inner = inner[: len(inner) - len(moved)]
            for place, number in enumerate(moved):
                ends = (inner[number], near[place]) if number < first_out else (near[place], inner[number])
                copies[number] = pltpu.make_async_copy(*ends, sems.at[place])
                inner[number] = near[place]
        for number in away:
            copies[number].start()
        for number in away:
            copies[number].wait()
        kernel(*inner)
        for number in moved[len(away) :]:
            copies[number].start()
        for number in moved[len(away) :]:
            copies[number].wait()

    def space(number):
        array = arrays[number]
        zeros = (0,) * len(array.shape)
        if number in moved:
            return pl.BlockSpec(memory_space=pltpu.HBM)
        if any(array is other for other in resident):
            return pl.BlockSpec(memory_space=pltpu.VMEM)
        if array is counts:
            return pl.BlockSpec(memory_space=pltpu.SMEM)
        return pl.BlockSpec(array.shape, lambda i: zeros)

    near = [pltpu.VMEM(arrays[number].shape, arrays[number].dtype) for number in moved]
    operands = [
        pltpu.with_memory_space_constraint(array, pltpu.HBM) if number in away else array
        for number, array in enumerate(operands)
    ]
    return pl.pallas_call(
        moving,
        out_shape=[
            pltpu.HBM(out.shape, out.dtype) if number in stored else out for number, out in enumerate(out_shape)
        ],
        grid=(1,),
        in_specs=[space(number) for number in range(first_out)],
        out_specs=[space(first_out + number) for number in range(len(out_shape))],
        scratch_shapes=[*scratch, *near] + ([pltpu.SemaphoreType.DMA((len(moved),))] if moved else []),
        cost_estimate=pl.CostEstimate(flops=flops, bytes_accessed=flops // 300, transcendentals=0),
        compiler_params=pltpu.CompilerParams(vmem_limit_bytes=vmem * 1024 * 1024),
        name=name,
    )(*operands)


def shape(dims, kind):
    return jax.ShapeDtypeStruct(dims, kind)


def swap_exp(block, step, exp_count):
    if step == 0:
        return block
    return lax.ppermute(block, "exp", [(i, i ^ step) for i in range(exp_count)])


def swap_core(block, rep_count):
    return lax.ppermute(block, "rep", [(i, i ^ 1) for i in range(rep_count)])


def swap_chip(block, step, rep_count):
    if step == 0:
        return block
    return lax.ppermute(block, "rep", [(i, i ^ (2 * step)) for i in range(rep_count)])


def upright(row):
    count = row.shape[1]
    same = lax.broadcasted_iota(i32, (count, count), 0) == lax.broadcasted_iota(i32, (count, count), 1)
    return jnp.sum(jnp.where(same, row, jnp.zeros_like(row)), axis=1, keepdims=True)


def one_hot(spots):
    return spots.astype(f32).astype(bf16)


def slot_spots(capacity, padded, exp_count, routes):
    tokens = routes.shape[1]
    block = jnp.bitwise_xor(upright(routes[...]), lax.axis_index("exp"))
    chosen = block == lax.broadcasted_iota(i32, (tokens, exp_count), 1)
    above = lax.broadcasted_iota(i32, (tokens, tokens), 1) < lax.broadcasted_iota(i32, (tokens, tokens), 0)
    ranks = dot(one_hot(above), one_hot(chosen))
    rank = jnp.sum(jnp.where(chosen, ranks, 0.0), axis=1, keepdims=True).astype(i32)
    target = block * padded + rank
    return one_hot(target == lax.broadcasted_iota(i32, (tokens, exp_count * padded), 1))


def prepare_kernel(fetch_slots, capacity, padded, exp_count, counts, routes, pick, pick_swapped, home):
    tokens = routes.shape[1]
    rep_count = counts.shape[1]
    replica = lax.axis_index("rep")
    position = lax.broadcasted_iota(i32, (tokens, 1), 0)
    source = jnp.zeros((tokens, 1), i32)
    start = jnp.zeros((tokens, 1), i32)
    end = jnp.int32(0)
    for shard in range(rep_count):
        end = end + counts[0, shard]
        passed = position >= end
        source = source + passed.astype(i32)
        start = jnp.where(passed, end, start)
    home_of = slot_spots(capacity, padded, exp_count, routes)
    home[...] = home_of

    places = lax.broadcasted_iota(i32, (tokens, rep_count * fetch_slots), 1)
    for shard, matrix in ((source, pick), (jnp.bitwise_xor(source, replica), pick_swapped)):
        place = shard * fetch_slots + position - start
        matrix[...] = dot(home_of, one_hot(place == places), ((0,), (0,))).astype(bf16)


def part_of(chunk, width):
    return slice(chunk * width, (chunk + 1) * width)


def serve(table, rows, asking):
    fetch_slots = table.shape[2]
    asked = jnp.concatenate([table[0, pl.ds(replica, 1), :] for replica in asking], axis=1)
    chosen = asked == lax.broadcasted_iota(i32, (rows.shape[0], asked.shape[1]), 0)
    found = dot(one_hot(chosen), rows, ((0,), (0,))).astype(bf16)
    return [found[number * fetch_slots : (number + 1) * fetch_slots] for number in range(len(asking))]


def begin_kernel(capacity, padded, table_far, rows_far, routes_far, weight_far, grads_far, *refs):
    served_far, *sent = refs[:-7]
    table, rows, routes, weight, grads, served, sems = refs[-7:]
    width = served.shape[2]
    fetches = [
        pltpu.make_async_copy(far, near, sems.at[number])
        for number, (far, near) in enumerate(
            (
                (table_far, table),
                (rows_far.at[:, :width], rows),
                (routes_far, routes),
                (weight_far, weight),
                (grads_far, grads),
            )
        )
    ]
    store = pltpu.make_async_copy(served, served_far, sems.at[5])
    for copy in fetches:
        copy.start()
    for copy in fetches[:2]:
        copy.wait()
    for replica, found in enumerate(serve(table, rows[...], range(served.shape[0]))):
        served[replica] = found
    store.start()
    for copy in fetches[2:]:
        copy.wait()
    home = slot_spots(capacity, padded, len(sent), routes)
    scaled = (upright(weight[...]) * grads[...].astype(f32)).astype(bf16)
    by_slot = dot(home, scaled, ((0,), (0,))).astype(bf16)
    for step in range(len(sent)):
        sent[step][...] = by_slot[step * padded : step * padded + capacity]
    store.wait()


def serve_last_kernel(own_table, own_rows, pair_table, pair_rows, *served):
    fetch_slots = own_table.shape[2]
    width = served[0].shape[1]
    asking = [jnp.bitwise_xor(lax.axis_index("rep"), 2 * step) for step in range(len(served))]
    for table, rows, base in ((own_table, own_rows, 0), (pair_table, pair_rows, fetch_slots)):
        for block, found in zip(served, serve(table, rows[:, rows.shape[1] - width :], asking)):
            block[base : base + fetch_slots] = found


def pick_first_kernel(capacity, padded, pick, arrived, *refs):
    exp_count = (len(refs) - 3) // 2
    grads, refs = refs[:exp_count], refs[exp_count:]
    sent_far, grads_far, (sent, sems) = refs[0], refs[1 : exp_count + 1], refs[exp_count + 1 :]
    put_away = [
        pltpu.make_async_copy(block, place, sems.at[exp_count + step])
        for step, (block, place) in enumerate(zip(grads, grads_far))
    ]
    for copy in put_away:
        copy.start()
    shards, rows, width = arrived.shape
    by_slot = dot(pick[...], arrived[...].reshape(shards * rows, width)).astype(bf16)
    column = lax.axis_index("exp")
    for step in range(exp_count):
        sent[step] = by_slot[step * padded : step * padded + capacity]
        copy = pltpu.make_async_copy(sent.at[step], sent_far.at[jnp.bitwise_xor(column, step)], sems.at[step])
        copy.start()
        put_away.append(copy)
    for copy in put_away:
        copy.wait()


def pick_last_kernel(capacity, padded, chips, pick, *refs):
    arrived, sent = refs[:chips], refs[chips:]
    rows = jnp.concatenate([block[...] for block in arrived], axis=0)
    by_slot = dot(pick[...], rows).astype(bf16)
    for step in range(len(sent)):
        sent[step][...] = by_slot[step * padded : step * padded + capacity]


def fill(tile, blocks, capacity, padded):
    tile[...] = jnp.zeros(tile.shape, tile.dtype)
    for step, block in enumerate(blocks):
        tile[step * padded : step * padded + capacity, :] = block[...]


def partial_kernel(capacity, padded, gate, down, arrived, turned, pre_act, adapted, tile):
    column = lax.axis_index("exp")
    tile[...] = jnp.zeros(tile.shape, tile.dtype)
    for step in range(arrived.shape[0]):
        tile[step * padded : step * padded + capacity, :] = arrived[jnp.bitwise_xor(column, step)]
    width = tile.shape[1]
    pre_act[...] = dot(tile[...], gate[0, :width])
    adapted[...] = dot(tile[...], down[0, :width])
    turned[...] = tile[...].T


def fetch_kernel(*refs):
    count = (len(refs) - 1) // 2
    sems = refs[-1]
    copies = [pltpu.make_async_copy(refs[i], refs[count + i], sems.at[i]) for i in range(count)]
    for copy in copies:
        copy.start()
    for copy in copies:
        copy.wait()


def forward(rows, pre_first, adapted_first, grads, gate, down, up):
    width = gate.shape[1] - rows.shape[1]
    adapted = (adapted_first + dot(rows, down[0, width:])).astype(bf16)
    pre_act = pre_first + dot(rows, gate[0, width:]) + dot(adapted, up[0])
    gate_value = jax.nn.sigmoid(pre_act)
    activated = (pre_act * gate_value).astype(bf16)
    slope = gate_value * (1.0 + pre_act * (1.0 - gate_value))
    grad_pre = (grads.astype(f32) * slope).astype(bf16)
    back = dot(grad_pre, up[0], ((1,), (1,))).astype(bf16)
    return activated, adapted, grad_pre, back


def early_kernel(capacity, padded, steps, pre_first, adapted_first, gate, down, up, *refs):
    blocks, refs = refs[:steps], refs[steps:]
    grads, refs = refs[:steps], refs[steps:]
    activated, refs = refs[:steps], refs[steps:]
    turned, adapted, grad_pre, back, tile, grad_tile = refs
    fill(tile, blocks, capacity, padded)
    fill(grad_tile, grads, capacity, padded)
    count = tile.shape[0]
    rows, adapted[...], grad_pre[...], back[...] = forward(
        tile[...], pre_first[:count], adapted_first[:count], grad_tile[...], gate, down, up
    )
    for step in range(steps):
        activated[step][...] = rows[step * padded : step * padded + capacity]
    turned[...] = tile[...].T


def late_kernel(
    capacity,
    padded,
    steps,
    turned_first,
    turned_early,
    adapted_early,
    grad_early,
    back_early,
    pre_first,
    adapted_first,
    gate,
    down,
    up,
    *refs,
):
    blocks, refs = refs[:steps], refs[steps:]
    grads, refs = refs[:steps], refs[steps:]
    activated, refs = refs[:steps], refs[steps:]
    keep, give, tile, grad_tile, down_term, up_term = refs
    fill(tile, blocks, capacity, padded)
    fill(grad_tile, grads, capacity, padded)
    count = pre_first.shape[0] - tile.shape[0]
    rows, adapted, grad_pre, back = forward(
        tile[...], pre_first[count:], adapted_first[count:], grad_tile[...], gate, down, up
    )
    for step in range(steps):
        activated[step][...] = rows[step * padded : step * padded + capacity]
    width = turned_first.shape[0]
    down_term[:width] = dot(turned_first[...], jnp.concatenate([back_early[...], back], axis=0))
    down_term[width:] = dot(turned_early[...], back_early[...]) + dot(tile[...], back, ((0,), (0,)))
    owners, up_rows, hidden_units = up_term.shape
    part = dot(
        jnp.concatenate([adapted_early[...], adapted], axis=0),
        jnp.concatenate([grad_early[...], grad_pre], axis=0),
        ((0,), (0,)),
    )
    for owner in range(owners):
        up_term[owner] = part[owner * up_rows : (owner + 1) * up_rows]

    pairs, _, lanes = keep.shape
    down_rows = down_term.shape[0] // owners
    replica = lax.axis_index("rep")
    for chip in range(pairs):
        for flip, target in ((0, keep), (1, give)):
            owner = jnp.bitwise_xor(replica, 2 * chip + flip)
            mine = down_term[pl.ds(pl.multiple_of(owner * down_rows, 8), down_rows)]
            target[chip, :down_rows] = mine.astype(target.dtype)
            mine = up_term[owner].astype(target.dtype)
            for part in range(hidden_units // lanes):
                base = down_rows + part * up_rows
                target[chip, base : base + up_rows] = mine[:, part * lanes : (part + 1) * lanes]


def end_kernel(capacity, padded, home, weight, kept, came, *refs):
    *blocks, down_grad, up_grad, out, tile = refs
    total = kept[...].astype(f32) + came[...].astype(f32)
    down_rows = down_grad.shape[1]
    up_rows, hidden_units = up_grad.shape[1:]
    lanes = total.shape[1]
    down_grad[0] = total[:down_rows]
    for part in range(hidden_units // lanes):
        base = down_rows + part * up_rows
        up_grad[0, :, part * lanes : (part + 1) * lanes] = total[base : base + up_rows]
    fill(tile, blocks, capacity, padded)
    out[...] = (upright(weight[...]) * dot(home[...], tile[...])).astype(bf16)


def body(
    replay_buffer_rows,
    shard_request_index,
    replica_fetch_count,
    routes,
    router_route_weight,
    output_gradient,
    frozen_gate_weight,
    adapter_down_weight,
    adapter_up_weight,
):
    rep_count = lax.axis_size("rep")
    exp_count = lax.axis_size("exp")
    pairs = rep_count // 2
    token_count = routes.shape[0]
    shard_rows, model_width = replay_buffer_rows.shape
    fetch_slots = shard_request_index.shape[2]
    hidden_units = frozen_gate_weight.shape[2]
    rank_width = adapter_down_weight.shape[2]
    capacity = 7 * token_count // (4 * exp_count)
    padded = -(-capacity // 16) * 16
    slots = exp_count * padded
    fetched_rows = rep_count * fetch_slots
    first_width = model_width // 128 * FIRST_PART // PARTS * 128
    last_width = model_width - first_width

    routes_row = routes.reshape(1, token_count)
    weight_row = router_route_weight.reshape(1, token_count)

    pair_rows = swap_core(replay_buffer_rows, rep_count)
    pair_table = swap_core(shard_request_index, rep_count)
    operands = [shard_request_index, replay_buffer_rows, routes_row, weight_row, output_gradient]
    far = pl.BlockSpec(memory_space=pltpu.HBM)
    near = pl.BlockSpec(memory_space=pltpu.VMEM)
    served, *grads = pl.pallas_call(
        functools.partial(begin_kernel, capacity, padded),
        out_shape=[pltpu.HBM((rep_count, fetch_slots, first_width), bf16)]
        + [shape((capacity, hidden_units), bf16)] * exp_count,
        in_specs=[far] * len(operands),
        out_specs=[far] + [near] * exp_count,
        scratch_shapes=[
            pltpu.VMEM(shard_request_index.shape, i32),
            pltpu.VMEM((shard_rows, first_width), bf16),
            pltpu.VMEM(routes_row.shape, i32),
            pltpu.VMEM(weight_row.shape, f32),
            pltpu.VMEM(output_gradient.shape, bf16),
            pltpu.VMEM((rep_count, fetch_slots, first_width), bf16),
            pltpu.SemaphoreType.DMA((6,)),
        ],
        compiler_params=pltpu.CompilerParams(vmem_limit_bytes=16 * 1024 * 1024),
        name="begin",
    )(*[pltpu.with_memory_space_constraint(array, pltpu.HBM) for array in operands])
    served, routes_row, pair_rows, pair_table = lax.optimization_barrier((served, routes_row, pair_rows, pair_table))
    arrived = lax.all_to_all(served, "rep", 0, 0, tiled=True)
    grads = [swap_exp(block, step, exp_count) for step, block in enumerate(grads)]
    routes_row, grads[1] = lax.optimization_barrier((routes_row, grads[1]))
    pick, pick_swapped, home = call(
        functools.partial(prepare_kernel, fetch_slots, capacity, padded, exp_count),
        [shape((slots, fetched_rows), bf16)] * 2 + [shape((token_count, slots), bf16)],
        [replica_fetch_count, routes_row],
        counts=replica_fetch_count,
        stored=[1, 2],
        flops=4 * token_count * slots * fetched_rows,
        name="prepare",
    )
    sent, *grads = pl.pallas_call(
        functools.partial(pick_first_kernel, capacity, padded),
        out_shape=[pltpu.HBM((exp_count, capacity, first_width), bf16)]
        + [pltpu.HBM((capacity, hidden_units), bf16)] * exp_count,
        in_specs=[near] * (2 + exp_count),
        out_specs=[far] * (1 + exp_count),
        scratch_shapes=[
            pltpu.VMEM((exp_count, capacity, first_width), bf16),
            pltpu.SemaphoreType.DMA((2 * exp_count,)),
        ],
        compiler_params=pltpu.CompilerParams(vmem_limit_bytes=16 * 1024 * 1024),
        name="pick_first",
    )(pick, arrived, *grads)

    pair_rows, sent = lax.optimization_barrier((pair_rows, sent))
    first_blocks = lax.all_to_all(sent, "exp", 0, 0, tiled=True)
    served = call(
        serve_last_kernel,
        [shape((2 * fetch_slots, last_width), bf16)] * pairs,
        [shard_request_index, replay_buffer_rows, pair_table, pair_rows],
        far=[shard_request_index, pair_table],
        flops=2 * fetched_rows * shard_rows * last_width,
        name="serve_last",
    )
    arrived = [swap_chip(block, step, rep_count) for step, block in enumerate(served)]
    first_sent, *sent = call(
        functools.partial(pick_last_kernel, capacity, padded, pairs),
        [shape((capacity, last_width), bf16)] * exp_count,
        [pick_swapped, *arrived],
        flops=2 * slots * fetched_rows * last_width,
        name="pick_last",
    )
    weights = [frozen_gate_weight, adapter_down_weight, adapter_up_weight]
    first_sent, *weights = lax.optimization_barrier((first_sent, *weights))
    weights = pl.pallas_call(
        fetch_kernel,
        out_shape=[pltpu.VMEM(array.shape, array.dtype) for array in weights],
        in_specs=[far] * len(weights),
        out_specs=[near] * len(weights),
        scratch_shapes=[pltpu.SemaphoreType.DMA((len(weights),))],
        compiler_params=pltpu.CompilerParams(vmem_limit_bytes=16 * 1024 * 1024),
        name="fetch",
    )(*[pltpu.with_memory_space_constraint(array, pltpu.HBM) for array in weights])
    weights = [pltpu.with_memory_space_constraint(array, pltpu.VMEM) for array in weights]
    last_blocks = [swap_exp(block, step, exp_count) for step, block in enumerate((first_sent, *sent))]

    turned, pre_first, adapted_first = call(
        functools.partial(partial_kernel, capacity, padded),
        [shape((first_width, slots), bf16), shape((slots, hidden_units), f32), shape((slots, rank_width), f32)],
        [*weights[:2], first_blocks],
        resident=weights,
        scratch=[pltpu.VMEM((slots, first_width), bf16)],
        flops=2 * slots * first_width * (hidden_units + rank_width),
        name="partial",
    )

    term_rows = (model_width + rank_width * hidden_units // rank_width) // rep_count
    steps = exp_count // 2
    count = steps * padded
    *activated, turned_early, adapted_early, grad_early, back_early = call(
        functools.partial(early_kernel, capacity, padded, steps),
        [shape((capacity, hidden_units), bf16)] * steps
        + [
            shape((last_width, count), bf16),
            shape((count, rank_width), bf16),
            shape((count, hidden_units), bf16),
            shape((count, rank_width), bf16),
        ],
        [pre_first, adapted_first, *weights, *last_blocks[:steps], *grads[:steps]],
        resident=weights,
        scratch=[pltpu.VMEM((count, last_width), bf16), pltpu.VMEM((count, hidden_units), bf16)],
        flops=2 * count * last_width * (hidden_units + rank_width),
        name="early",
    )
    count = slots - count
    *late, keep, give = call(
        functools.partial(late_kernel, capacity, padded, exp_count - steps),
        [shape((capacity, hidden_units), bf16)] * (exp_count - steps)
        + [shape((pairs, term_rows, rank_width), kind) for kind in (f32, bf16)],
        [
            turned,
            turned_early,
            adapted_early,
            grad_early,
            back_early,
            pre_first,
            adapted_first,
            *weights,
            *last_blocks[steps:],
            *grads[steps:],
        ],
        resident=weights,
        scratch=[
            pltpu.VMEM((count, last_width), bf16),
            pltpu.VMEM((count, hidden_units), bf16),
            pltpu.VMEM((model_width, rank_width), f32),
            pltpu.VMEM((rep_count, rank_width // rep_count, hidden_units), f32),
        ],
        flops=2 * count * last_width * (hidden_units + rank_width) + 4 * slots * model_width * rank_width,
        name="late",
    )
    activated += late

    pair_terms = swap_core(give, rep_count)
    results = [swap_exp(block, step, exp_count) for step, block in enumerate(activated)]
    terms = keep + pair_terms.astype(f32)
    while terms.shape[0] > 2:
        half = terms.shape[0] // 2
        terms = terms[:half] + swap_chip(terms[half:].astype(bf16), half, rep_count).astype(f32)
    down_grad, up_grad, out_rows = call(
        functools.partial(end_kernel, capacity, padded),
        [
            shape((1, model_width // rep_count, rank_width), f32),
            shape((1, rank_width // rep_count, hidden_units), f32),
            shape((token_count, hidden_units), bf16),
        ],
        [home, weight_row, terms[0], swap_chip(terms[1].astype(bf16), 1, rep_count), *results],
        scratch=[pltpu.VMEM((slots, hidden_units), bf16)],
        flops=2 * token_count * slots * hidden_units,
        name="end",
    )
    return (out_rows, down_grad, up_grad)


def solution(mesh):
    placed = (
        P(("rep", "exp"), None),
        P(("rep", "exp"), None, None),
        P(("rep", "exp"), None),
        P(("rep", "exp"), None),
        P(("rep", "exp"), None),
        P(("rep", "exp"), None),
        P("exp", None, None),
        P("exp", None, None),
        P("exp", None, None),
    )
    return jax.shard_map(
        body,
        mesh=mesh,
        in_specs=placed,
        out_specs=(P(("rep", "exp"), None), P("exp", "rep", None), P("exp", "rep", None)),
        check_vma=False,
    )
```

```python
import functools

import jax
import jax.numpy as jnp
from jax import lax
from jax.experimental import pallas as pl
from jax.experimental.pallas import tpu as pltpu
from jax.sharding import PartitionSpec as P

FIRST_PART = 13
PARTS = 28
bf16 = jnp.bfloat16
f32 = jnp.float32
i32 = jnp.int32


def dot(a, b, contract=((1,), (0,))):
    return lax.dot_general(a, b, (contract, ((), ())), preferred_element_type=f32)


def call(kernel, out_shape, operands, counts=None, resident=(), far=(), stored=(), scratch=(), flops=0, vmem=16, name=None):
    first_out = len(operands)
    away = [number for number, array in enumerate(operands) if any(array is other for other in far)]
    moved = [*away, *(first_out + number for number in stored)]
    arrays = [*operands, *out_shape]

    def moving(*refs):
        inner = list(refs)
        copies = {}
        if moved:
            *inner, sems = inner
            near = inner[len(inner) - len(moved) :]
            inner = inner[: len(inner) - len(moved)]
            for place, number in enumerate(moved):
                ends = (inner[number], near[place]) if number < first_out else (near[place], inner[number])
                copies[number] = pltpu.make_async_copy(*ends, sems.at[place])
                inner[number] = near[place]
        for number in away:
            copies[number].start()
        for number in away:
            copies[number].wait()
        kernel(*inner)
        for number in moved[len(away) :]:
            copies[number].start()
        for number in moved[len(away) :]:
            copies[number].wait()

    def space(number):
        array = arrays[number]
        zeros = (0,) * len(array.shape)
        if number in moved:
            return pl.BlockSpec(memory_space=pltpu.HBM)
        if any(array is other for other in resident):
            return pl.BlockSpec(memory_space=pltpu.VMEM)
        if array is counts:
            return pl.BlockSpec(memory_space=pltpu.SMEM)
        return pl.BlockSpec(array.shape, lambda i: zeros)

    near = [pltpu.VMEM(arrays[number].shape, arrays[number].dtype) for number in moved]
    operands = [
        pltpu.with_memory_space_constraint(array, pltpu.HBM) if number in away else array
        for number, array in enumerate(operands)
    ]
    return pl.pallas_call(
        moving,
        out_shape=[
            pltpu.HBM(out.shape, out.dtype) if number in stored else out for number, out in enumerate(out_shape)
        ],
        grid=(1,),
        in_specs=[space(number) for number in range(first_out)],
        out_specs=[space(first_out + number) for number in range(len(out_shape))],
        scratch_shapes=[*scratch, *near] + ([pltpu.SemaphoreType.DMA((len(moved),))] if moved else []),
        cost_estimate=pl.CostEstimate(flops=flops, bytes_accessed=flops // 300, transcendentals=0),
        compiler_params=pltpu.CompilerParams(vmem_limit_bytes=vmem * 1024 * 1024),
        name=name,
    )(*operands)


def shape(dims, kind):
    return jax.ShapeDtypeStruct(dims, kind)


def swap_exp(block, step, exp_count):
    if step == 0:
        return block
    return lax.ppermute(block, "exp", [(i, i ^ step) for i in range(exp_count)])


def swap_all(blocks, exp_count):
    came = list(blocks)
    for step in [*range(exp_count // 2, exp_count), *range(1, exp_count // 2)]:
        came[step] = swap_exp(blocks[step], step, exp_count)
    return came


def swap_core(block, rep_count):
    return lax.ppermute(block, "rep", [(i, i ^ 1) for i in range(rep_count)])


def swap_chip(block, step, rep_count):
    if step == 0:
        return block
    return lax.ppermute(block, "rep", [(i, i ^ (2 * step)) for i in range(rep_count)])


def upright(row):
    count = row.shape[1]
    same = lax.broadcasted_iota(i32, (count, count), 0) == lax.broadcasted_iota(i32, (count, count), 1)
    return jnp.sum(jnp.where(same, row, jnp.zeros_like(row)), axis=1, keepdims=True)


def one_hot(spots):
    return spots.astype(f32).astype(bf16)


def slot_spots(capacity, padded, exp_count, routes):
    tokens = routes.shape[1]
    block = jnp.bitwise_xor(upright(routes[...]), lax.axis_index("exp"))
    chosen = block == lax.broadcasted_iota(i32, (tokens, exp_count), 1)
    above = lax.broadcasted_iota(i32, (tokens, tokens), 1) < lax.broadcasted_iota(i32, (tokens, tokens), 0)
    ranks = dot(one_hot(above), one_hot(chosen))
    rank = jnp.sum(jnp.where(chosen, ranks, 0.0), axis=1, keepdims=True).astype(i32)
    target = block * padded + rank
    return one_hot(target == lax.broadcasted_iota(i32, (tokens, exp_count * padded), 1))


def prepare_kernel(fetch_slots, capacity, padded, exp_count, counts, routes, pick, home):
    tokens = routes.shape[1]
    rep_count = counts.shape[1]
    replica = lax.axis_index("rep")
    position = lax.broadcasted_iota(i32, (tokens, 1), 0)
    source = jnp.zeros((tokens, 1), i32)
    start = jnp.zeros((tokens, 1), i32)
    end = jnp.int32(0)
    for shard in range(rep_count):
        end = end + counts[0, shard]
        passed = position >= end
        source = source + passed.astype(i32)
        start = jnp.where(passed, end, start)
    home_of = slot_spots(capacity, padded, exp_count, routes)
    home[...] = home_of

    places = lax.broadcasted_iota(i32, (tokens, rep_count * fetch_slots), 1)
    place = jnp.bitwise_xor(source, replica) * fetch_slots + position - start
    pick[...] = dot(home_of, one_hot(place == places), ((0,), (0,))).astype(bf16)


def part_of(chunk, width):
    return slice(chunk * width, (chunk + 1) * width)


def serve(table, rows, asking):
    fetch_slots = table.shape[2]
    asked = jnp.concatenate([table[0, pl.ds(replica, 1), :] for replica in asking], axis=1)
    chosen = asked == lax.broadcasted_iota(i32, (rows.shape[0], asked.shape[1]), 0)
    found = dot(one_hot(chosen), rows, ((0,), (0,))).astype(bf16)
    return [found[number * fetch_slots : (number + 1) * fetch_slots] for number in range(len(asking))]


def asking_chips(pairs):
    return [jnp.bitwise_xor(lax.axis_index("rep"), 2 * step) for step in range(pairs)]


def begin_kernel(capacity, padded, table_far, rows_far, routes_far, weight_far, grads_far, *refs):
    served, *sent = refs[:-6]
    table, rows, routes, weight, grads, sems = refs[-6:]
    width = rows.shape[1]
    fetches = [
        pltpu.make_async_copy(far, near, sems.at[number])
        for number, (far, near) in enumerate(
            (
                (routes_far, routes),
                (weight_far, weight),
                (grads_far, grads),
                (table_far, table),
                (rows_far.at[:, :width], rows),
            )
        )
    ]
    for copy in fetches:
        copy.start()
    for copy in fetches[:3]:
        copy.wait()
    home = slot_spots(capacity, padded, len(sent), routes)
    scaled = (upright(weight[...]) * grads[...].astype(f32)).astype(bf16)
    by_slot = dot(home, scaled, ((0,), (0,))).astype(bf16)
    for step in range(len(sent)):
        sent[step][...] = by_slot[step * padded : step * padded + capacity]
    for copy in fetches[3:]:
        copy.wait()
    for step, found in enumerate(serve(table, rows[...], asking_chips(served.shape[0]))):
        served[step] = found


def serve_first_kernel(table, rows, own, *served):
    fetch_slots = own.shape[1]
    width = own.shape[2]
    for step, found in enumerate(serve(table, rows[:, :width], asking_chips(len(served)))):
        served[step][:fetch_slots] = own[step]
        served[step][fetch_slots:] = found


def serve_last_kernel(own_table, own_rows, pair_table, pair_rows, *served):
    fetch_slots = own_table.shape[2]
    width = served[0].shape[1]
    asking = asking_chips(len(served))
    for table, rows, base in ((own_table, own_rows, 0), (pair_table, pair_rows, fetch_slots)):
        for block, found in zip(served, serve(table, rows[:, rows.shape[1] - width :], asking)):
            block[base : base + fetch_slots] = found


def pick_first_kernel(capacity, padded, chips, pick, *refs):
    arrived, refs = refs[:chips], refs[chips:]
    exp_count = (len(refs) - 3) // 2
    grads, refs = refs[:exp_count], refs[exp_count:]
    sent_far, grads_far, (sent, sems) = refs[0], refs[1 : exp_count + 1], refs[exp_count + 1 :]
    put_away = [
        pltpu.make_async_copy(block, place, sems.at[exp_count + step])
        for step, (block, place) in enumerate(zip(grads, grads_far))
    ]
    for copy in put_away:
        copy.start()
    rows = jnp.concatenate([block[...] for block in arrived], axis=0)
    by_slot = dot(pick[...], rows).astype(bf16)
    column = lax.axis_index("exp")
    for step in range(exp_count):
        sent[step] = by_slot[step * padded : step * padded + capacity]
        copy = pltpu.make_async_copy(sent.at[step], sent_far.at[jnp.bitwise_xor(column, step)], sems.at[step])
        copy.start()
        put_away.append(copy)
    for copy in put_away:
        copy.wait()


def pick_last_kernel(capacity, padded, chips, pick, *refs):
    arrived, sent = refs[:chips], refs[chips:]
    rows = jnp.concatenate([block[...] for block in arrived], axis=0)
    by_slot = dot(pick[...], rows).astype(bf16)
    for step in range(len(sent)):
        sent[step][...] = by_slot[step * padded : step * padded + capacity]


def fill(tile, blocks, capacity, padded):
    tile[...] = jnp.zeros(tile.shape, tile.dtype)
    for step, block in enumerate(blocks):
        tile[step * padded : step * padded + capacity, :] = block[...]


def partial_kernel(capacity, padded, gate, down, arrived, turned, pre_act, adapted, tile):
    column = lax.axis_index("exp")
    tile[...] = jnp.zeros(tile.shape, tile.dtype)
    for step in range(arrived.shape[0]):
        tile[step * padded : step * padded + capacity, :] = arrived[jnp.bitwise_xor(column, step)]
    width = tile.shape[1]
    pre_act[...] = dot(tile[...], gate[0, :width])
    adapted[...] = dot(tile[...], down[0, :width])
    turned[...] = tile[...].T


def fetch_kernel(*refs):
    count = (len(refs) - 1) // 2
    sems = refs[-1]
    copies = [pltpu.make_async_copy(refs[i], refs[count + i], sems.at[i]) for i in range(count)]
    for copy in copies:
        copy.start()
    for copy in copies:
        copy.wait()


def forward(rows, pre_first, adapted_first, grads, gate, down, up):
    width = gate.shape[1] - rows.shape[1]
    adapted = (adapted_first + dot(rows, down[0, width:])).astype(bf16)
    pre_act = pre_first + dot(rows, gate[0, width:]) + dot(adapted, up[0])
    gate_value = jax.nn.sigmoid(pre_act)
    activated = (pre_act * gate_value).astype(bf16)
    slope = gate_value * (1.0 + pre_act * (1.0 - gate_value))
    grad_pre = (grads.astype(f32) * slope).astype(bf16)
    back = dot(grad_pre, up[0], ((1,), (1,))).astype(bf16)
    return activated, adapted, grad_pre, back


def early_kernel(capacity, padded, steps, pre_first, adapted_first, gate, down, up, *refs):
    blocks, refs = refs[:steps], refs[steps:]
    grads, refs = refs[:steps], refs[steps:]
    activated, refs = refs[:steps], refs[steps:]
    turned, adapted, grad_pre, back, tile, grad_tile = refs
    fill(tile, blocks, capacity, padded)
    fill(grad_tile, grads, capacity, padded)
    count = tile.shape[0]
    rows, adapted[...], grad_pre[...], back[...] = forward(
        tile[...], pre_first[:count], adapted_first[:count], grad_tile[...], gate, down, up
    )
    for step in range(steps):
        activated[step][...] = rows[step * padded : step * padded + capacity]
    turned[...] = tile[...].T


def late_kernel(
    capacity,
    padded,
    steps,
    turned_first,
    turned_early,
    adapted_early,
    grad_early,
    back_early,
    pre_first,
    adapted_first,
    gate,
    down,
    up,
    *refs,
):
    blocks, refs = refs[:steps], refs[steps:]
    grads, refs = refs[:steps], refs[steps:]
    activated, refs = refs[:steps], refs[steps:]
    keep, give, tile, grad_tile, down_term, up_term = refs
    fill(tile, blocks, capacity, padded)
    fill(grad_tile, grads, capacity, padded)
    count = pre_first.shape[0] - tile.shape[0]
    rows, adapted, grad_pre, back = forward(
        tile[...], pre_first[count:], adapted_first[count:], grad_tile[...], gate, down, up
    )
    for step in range(steps):
        activated[step][...] = rows[step * padded : step * padded + capacity]
    width = turned_first.shape[0]
    down_term[:width] = dot(turned_first[...], jnp.concatenate([back_early[...], back], axis=0))
    down_term[width:] = dot(turned_early[...], back_early[...]) + dot(tile[...], back, ((0,), (0,)))
    owners, up_rows, hidden_units = up_term.shape
    part = dot(
        jnp.concatenate([adapted_early[...], adapted], axis=0),
        jnp.concatenate([grad_early[...], grad_pre], axis=0),
        ((0,), (0,)),
    )
    for owner in range(owners):
        up_term[owner] = part[owner * up_rows : (owner + 1) * up_rows]

    pairs, _, lanes = keep.shape
    down_rows = down_term.shape[0] // owners
    replica = lax.axis_index("rep")
    for chip in range(pairs):
        for flip, target in ((0, keep), (1, give)):
            owner = jnp.bitwise_xor(replica, 2 * chip + flip)
            mine = down_term[pl.ds(pl.multiple_of(owner * down_rows, 8), down_rows)]
            target[chip, :down_rows] = mine.astype(target.dtype)
            mine = up_term[owner].astype(target.dtype)
            for part in range(hidden_units // lanes):
                base = down_rows + part * up_rows
                target[chip, base : base + up_rows] = mine[:, part * lanes : (part + 1) * lanes]


def end_kernel(capacity, padded, home, weight, kept, came, *refs):
    *blocks, down_grad, up_grad, out, tile = refs
    total = kept[...].astype(f32) + came[...].astype(f32)
    down_rows = down_grad.shape[1]
    up_rows, hidden_units = up_grad.shape[1:]
    lanes = total.shape[1]
    down_grad[0] = total[:down_rows]
    for part in range(hidden_units // lanes):
        base = down_rows + part * up_rows
        up_grad[0, :, part * lanes : (part + 1) * lanes] = total[base : base + up_rows]
    fill(tile, blocks, capacity, padded)
    out[...] = (upright(weight[...]) * dot(home[...], tile[...])).astype(bf16)


def body(
    replay_buffer_rows,
    shard_request_index,
    replica_fetch_count,
    routes,
    router_route_weight,
    output_gradient,
    frozen_gate_weight,
    adapter_down_weight,
    adapter_up_weight,
):
    rep_count = lax.axis_size("rep")
    exp_count = lax.axis_size("exp")
    pairs = rep_count // 2
    token_count = routes.shape[0]
    shard_rows, model_width = replay_buffer_rows.shape
    fetch_slots = shard_request_index.shape[2]
    hidden_units = frozen_gate_weight.shape[2]
    rank_width = adapter_down_weight.shape[2]
    capacity = 7 * token_count // (4 * exp_count)
    padded = -(-capacity // 16) * 16
    slots = exp_count * padded
    fetched_rows = rep_count * fetch_slots
    first_width = model_width // 128 * FIRST_PART // PARTS * 128
    last_width = model_width - first_width

    routes_row = routes.reshape(1, token_count)
    weight_row = router_route_weight.reshape(1, token_count)

    pair_rows = swap_core(replay_buffer_rows, rep_count)
    pair_table = swap_core(shard_request_index, rep_count)
    operands = [shard_request_index, replay_buffer_rows, routes_row, weight_row, output_gradient]
    far = pl.BlockSpec(memory_space=pltpu.HBM)
    near = pl.BlockSpec(memory_space=pltpu.VMEM)
    served, *grads = pl.pallas_call(
        functools.partial(begin_kernel, capacity, padded),
        out_shape=[shape((pairs, fetch_slots, first_width), bf16)]
        + [shape((capacity, hidden_units), bf16)] * exp_count,
        in_specs=[far] * len(operands),
        out_specs=[near] * (1 + exp_count),
        scratch_shapes=[
            pltpu.VMEM(shard_request_index.shape, i32),
            pltpu.VMEM((shard_rows, first_width), bf16),
            pltpu.VMEM(routes_row.shape, i32),
            pltpu.VMEM(weight_row.shape, f32),
            pltpu.VMEM(output_gradient.shape, bf16),
            pltpu.SemaphoreType.DMA((5,)),
        ],
        compiler_params=pltpu.CompilerParams(vmem_limit_bytes=16 * 1024 * 1024),
        name="begin",
    )(*[pltpu.with_memory_space_constraint(array, pltpu.HBM) for array in operands])
    *grads, pair_table, pair_rows = lax.optimization_barrier((*grads, pair_table, pair_rows))
    served = call(
        serve_first_kernel,
        [shape((2 * fetch_slots, first_width), bf16)] * pairs,
        [pair_table, pair_rows, served],
        flops=2 * fetched_rows * shard_rows * first_width,
        name="serve_first",
    )
    *served, routes_row, pair_rows = lax.optimization_barrier((*served, routes_row, pair_rows))
    arrived = [swap_chip(block, step, rep_count) for step, block in enumerate(served)]
    grads = swap_all(grads, exp_count)
    pick, home = call(
        functools.partial(prepare_kernel, fetch_slots, capacity, padded, exp_count),
        [shape((slots, fetched_rows), bf16), shape((token_count, slots), bf16)],
        [replica_fetch_count, routes_row],
        counts=replica_fetch_count,
        stored=[1],
        flops=2 * token_count * slots * fetched_rows,
        name="prepare",
    )
    sent, *grads = pl.pallas_call(
        functools.partial(pick_first_kernel, capacity, padded, pairs),
        out_shape=[pltpu.HBM((exp_count, capacity, first_width), bf16)]
        + [pltpu.HBM((capacity, hidden_units), bf16)] * exp_count,
        in_specs=[near] * (1 + pairs + exp_count),
        out_specs=[far] * (1 + exp_count),
        scratch_shapes=[
            pltpu.VMEM((exp_count, capacity, first_width), bf16),
            pltpu.SemaphoreType.DMA((2 * exp_count,)),
        ],
        compiler_params=pltpu.CompilerParams(vmem_limit_bytes=16 * 1024 * 1024),
        name="pick_first",
    )(pick, *arrived, *grads[exp_count // 2 :], *grads[: exp_count // 2])
    grads = [*grads[exp_count // 2 :], *grads[: exp_count // 2]]

    pair_rows, sent = lax.optimization_barrier((pair_rows, sent))
    first_blocks = lax.all_to_all(sent, "exp", 0, 0, tiled=True)
    served = call(
        serve_last_kernel,
        [shape((2 * fetch_slots, last_width), bf16)] * pairs,
        [shard_request_index, replay_buffer_rows, pair_table, pair_rows],
        far=[shard_request_index, pair_table],
        flops=2 * fetched_rows * shard_rows * last_width,
        name="serve_last",
    )
    arrived = [swap_chip(block, step, rep_count) for step, block in enumerate(served)]
    first_sent, *sent = call(
        functools.partial(pick_last_kernel, capacity, padded, pairs),
        [shape((capacity, last_width), bf16)] * exp_count,
        [pick, *arrived],
        flops=2 * slots * fetched_rows * last_width,
        name="pick_last",
    )
    weights = [frozen_gate_weight, adapter_down_weight, adapter_up_weight]
    first_sent, *weights = lax.optimization_barrier((first_sent, *weights))
    weights = pl.pallas_call(
        fetch_kernel,
        out_shape=[pltpu.VMEM(array.shape, array.dtype) for array in weights],
        in_specs=[far] * len(weights),
        out_specs=[near] * len(weights),
        scratch_shapes=[pltpu.SemaphoreType.DMA((len(weights),))],
        compiler_params=pltpu.CompilerParams(vmem_limit_bytes=16 * 1024 * 1024),
        name="fetch",
    )(*[pltpu.with_memory_space_constraint(array, pltpu.HBM) for array in weights])
    weights = [pltpu.with_memory_space_constraint(array, pltpu.VMEM) for array in weights]
    last_blocks = swap_all([first_sent, *sent], exp_count)

    turned, pre_first, adapted_first = call(
        functools.partial(partial_kernel, capacity, padded),
        [shape((first_width, slots), bf16), shape((slots, hidden_units), f32), shape((slots, rank_width), f32)],
        [*weights[:2], first_blocks],
        resident=weights,
        scratch=[pltpu.VMEM((slots, first_width), bf16)],
        flops=2 * slots * first_width * (hidden_units + rank_width),
        name="partial",
    )

    term_rows = (model_width + rank_width * hidden_units // rank_width) // rep_count
    steps = exp_count // 2
    count = steps * padded
    *activated, turned_early, adapted_early, grad_early, back_early = call(
        functools.partial(early_kernel, capacity, padded, steps),
        [shape((capacity, hidden_units), bf16)] * steps
        + [
            shape((last_width, count), bf16),
            shape((count, rank_width), bf16),
            shape((count, hidden_units), bf16),
            shape((count, rank_width), bf16),
        ],
        [pre_first, adapted_first, *weights, *last_blocks[:steps], *grads[:steps]],
        resident=weights,
        scratch=[pltpu.VMEM((count, last_width), bf16), pltpu.VMEM((count, hidden_units), bf16)],
        flops=2 * count * last_width * (hidden_units + rank_width),
        name="early",
    )
    count = slots - count
    *late, keep, give = call(
        functools.partial(late_kernel, capacity, padded, exp_count - steps),
        [shape((capacity, hidden_units), bf16)] * (exp_count - steps)
        + [shape((pairs, term_rows, rank_width), kind) for kind in (f32, bf16)],
        [
            turned,
            turned_early,
            adapted_early,
            grad_early,
            back_early,
            pre_first,
            adapted_first,
            *weights,
            *last_blocks[steps:],
            *grads[steps:],
        ],
        resident=weights,
        scratch=[
            pltpu.VMEM((count, last_width), bf16),
            pltpu.VMEM((count, hidden_units), bf16),
            pltpu.VMEM((model_width, rank_width), f32),
            pltpu.VMEM((rep_count, rank_width // rep_count, hidden_units), f32),
        ],
        flops=2 * count * last_width * (hidden_units + rank_width) + 4 * slots * model_width * rank_width,
        name="late",
    )
    activated += late

    pair_terms = swap_core(give, rep_count)
    results = swap_all(activated, exp_count)
    terms = keep + pair_terms.astype(f32)
    while terms.shape[0] > 2:
        half = terms.shape[0] // 2
        terms = terms[:half] + swap_chip(terms[half:].astype(bf16), half, rep_count).astype(f32)
    down_grad, up_grad, out_rows = call(
        functools.partial(end_kernel, capacity, padded),
        [
            shape((1, model_width // rep_count, rank_width), f32),
            shape((1, rank_width // rep_count, hidden_units), f32),
            shape((token_count, hidden_units), bf16),
        ],
        [home, weight_row, terms[0], swap_chip(terms[1].astype(bf16), 1, rep_count), *results],
        scratch=[pltpu.VMEM((slots, hidden_units), bf16)],
        flops=2 * token_count * slots * hidden_units,
        name="end",
    )
    return (out_rows, down_grad, up_grad)


def solution(mesh):
    placed = (
        P(("rep", "exp"), None),
        P(("rep", "exp"), None, None),
        P(("rep", "exp"), None),
        P(("rep", "exp"), None),
        P(("rep", "exp"), None),
        P(("rep", "exp"), None),
        P("exp", None, None),
        P("exp", None, None),
        P("exp", None, None),
    )
    return jax.shard_map(
        body,
        mesh=mesh,
        in_specs=placed,
        out_specs=(P(("rep", "exp"), None), P("exp", "rep", None), P("exp", "rep", None)),
        check_vma=False,
    )
```

```python
import functools

import jax
import jax.numpy as jnp
from jax import lax
from jax.experimental import pallas as pl
from jax.experimental.pallas import tpu as pltpu
from jax.sharding import PartitionSpec as P

FIRST_PART = 13
PARTS = 28
bf16 = jnp.bfloat16
f32 = jnp.float32
i32 = jnp.int32


def dot(a, b, contract=((1,), (0,))):
    return lax.dot_general(a, b, (contract, ((), ())), preferred_element_type=f32)


def call(kernel, out_shape, operands, counts=None, resident=(), far=(), stored=(), scratch=(), flops=0, vmem=16, name=None):
    first_out = len(operands)
    away = [number for number, array in enumerate(operands) if any(array is other for other in far)]
    moved = [*away, *(first_out + number for number in stored)]
    arrays = [*operands, *out_shape]

    def moving(*refs):
        inner = list(refs)
        copies = {}
        if moved:
            *inner, sems = inner
            near = inner[len(inner) - len(moved) :]
            inner = inner[: len(inner) - len(moved)]
            for place, number in enumerate(moved):
                ends = (inner[number], near[place]) if number < first_out else (near[place], inner[number])
                copies[number] = pltpu.make_async_copy(*ends, sems.at[place])
                inner[number] = near[place]
        for number in away:
            copies[number].start()
        for number in away:
            copies[number].wait()
        kernel(*inner)
        for number in moved[len(away) :]:
            copies[number].start()
        for number in moved[len(away) :]:
            copies[number].wait()

    def space(number):
        array = arrays[number]
        zeros = (0,) * len(array.shape)
        if number in moved:
            return pl.BlockSpec(memory_space=pltpu.HBM)
        if any(array is other for other in resident):
            return pl.BlockSpec(memory_space=pltpu.VMEM)
        if array is counts:
            return pl.BlockSpec(memory_space=pltpu.SMEM)
        return pl.BlockSpec(array.shape, lambda i: zeros)

    near = [pltpu.VMEM(arrays[number].shape, arrays[number].dtype) for number in moved]
    operands = [
        pltpu.with_memory_space_constraint(array, pltpu.HBM) if number in away else array
        for number, array in enumerate(operands)
    ]
    return pl.pallas_call(
        moving,
        out_shape=[
            pltpu.HBM(out.shape, out.dtype) if number in stored else out for number, out in enumerate(out_shape)
        ],
        grid=(1,),
        in_specs=[space(number) for number in range(first_out)],
        out_specs=[space(first_out + number) for number in range(len(out_shape))],
        scratch_shapes=[*scratch, *near] + ([pltpu.SemaphoreType.DMA((len(moved),))] if moved else []),
        cost_estimate=pl.CostEstimate(flops=flops, bytes_accessed=flops // 300, transcendentals=0),
        compiler_params=pltpu.CompilerParams(vmem_limit_bytes=vmem * 1024 * 1024),
        name=name,
    )(*operands)


def shape(dims, kind):
    return jax.ShapeDtypeStruct(dims, kind)


def swap_exp(block, step, exp_count):
    if step == 0:
        return block
    return lax.ppermute(block, "exp", [(i, i ^ step) for i in range(exp_count)])


def swap_all(blocks, exp_count):
    came = list(blocks)
    for step in [*range(exp_count // 2, exp_count), *range(1, exp_count // 2)]:
        came[step] = swap_exp(blocks[step], step, exp_count)
    return came


def swap_core(block, rep_count):
    return lax.ppermute(block, "rep", [(i, i ^ 1) for i in range(rep_count)])


def swap_chip(block, step, rep_count):
    if step == 0:
        return block
    return lax.ppermute(block, "rep", [(i, i ^ (2 * step)) for i in range(rep_count)])


def upright(row):
    count = row.shape[1]
    same = lax.broadcasted_iota(i32, (count, count), 0) == lax.broadcasted_iota(i32, (count, count), 1)
    return jnp.sum(jnp.where(same, row, jnp.zeros_like(row)), axis=1, keepdims=True)


def one_hot(spots):
    return spots.astype(f32).astype(bf16)


def slot_spots(capacity, padded, exp_count, routes):
    tokens = routes.shape[1]
    block = jnp.bitwise_xor(upright(routes[...]), lax.axis_index("exp"))
    chosen = block == lax.broadcasted_iota(i32, (tokens, exp_count), 1)
    above = lax.broadcasted_iota(i32, (tokens, tokens), 1) < lax.broadcasted_iota(i32, (tokens, tokens), 0)
    ranks = dot(one_hot(above), one_hot(chosen))
    rank = jnp.sum(jnp.where(chosen, ranks, 0.0), axis=1, keepdims=True).astype(i32)
    target = block * padded + rank
    return one_hot(target == lax.broadcasted_iota(i32, (tokens, exp_count * padded), 1))


def prepare_kernel(fetch_slots, capacity, padded, exp_count, counts, routes, pick, home):
    tokens = routes.shape[1]
    rep_count = counts.shape[1]
    replica = lax.axis_index("rep")
    position = lax.broadcasted_iota(i32, (tokens, 1), 0)
    source = jnp.zeros((tokens, 1), i32)
    start = jnp.zeros((tokens, 1), i32)
    end = jnp.int32(0)
    for shard in range(rep_count):
        end = end + counts[0, shard]
        passed = position >= end
        source = source + passed.astype(i32)
        start = jnp.where(passed, end, start)
    home_of = slot_spots(capacity, padded, exp_count, routes)
    home[...] = home_of

    places = lax.broadcasted_iota(i32, (tokens, rep_count * fetch_slots), 1)
    place = jnp.bitwise_xor(source, replica) * fetch_slots + position - start
    pick[...] = dot(home_of, one_hot(place == places), ((0,), (0,))).astype(bf16)


def part_of(chunk, width):
    return slice(chunk * width, (chunk + 1) * width)


def serve(table, rows, asking):
    fetch_slots = table.shape[2]
    asked = jnp.concatenate([table[0, pl.ds(replica, 1), :] for replica in asking], axis=1)
    chosen = asked == lax.broadcasted_iota(i32, (rows.shape[0], asked.shape[1]), 0)
    found = dot(one_hot(chosen), rows, ((0,), (0,))).astype(bf16)
    return [found[number * fetch_slots : (number + 1) * fetch_slots] for number in range(len(asking))]


def asking_chips(pairs):
    return [jnp.bitwise_xor(lax.axis_index("rep"), 2 * step) for step in range(pairs)]


def begin_kernel(capacity, padded, table_far, rows_far, routes_far, weight_far, grads_far, *refs):
    served, *sent = refs[:-6]
    table, rows, routes, weight, grads, sems = refs[-6:]
    width = rows.shape[1]
    fetches = [
        pltpu.make_async_copy(far, near, sems.at[number])
        for number, (far, near) in enumerate(
            (
                (routes_far, routes),
                (weight_far, weight),
                (grads_far, grads),
                (table_far, table),
                (rows_far.at[:, :width], rows),
            )
        )
    ]
    for copy in fetches:
        copy.start()
    for copy in fetches[:3]:
        copy.wait()
    home = slot_spots(capacity, padded, len(sent), routes)
    scaled = (upright(weight[...]) * grads[...].astype(f32)).astype(bf16)
    by_slot = dot(home, scaled, ((0,), (0,))).astype(bf16)
    for step in range(len(sent)):
        sent[step][...] = by_slot[step * padded : step * padded + capacity]
    for copy in fetches[3:]:
        copy.wait()
    for step, found in enumerate(serve(table, rows[...], asking_chips(served.shape[0]))):
        served[step] = found


def serve_first_kernel(table, rows, own, *served):
    fetch_slots = own.shape[1]
    width = own.shape[2]
    for step, found in enumerate(serve(table, rows[:, :width], asking_chips(len(served)))):
        served[step][:fetch_slots] = own[step]
        served[step][fetch_slots:] = found


def serve_last_kernel(own_table, own_rows, pair_table, pair_rows, *served):
    fetch_slots = own_table.shape[2]
    width = served[0].shape[1]
    asking = asking_chips(len(served))
    for table, rows, base in ((own_table, own_rows, 0), (pair_table, pair_rows, fetch_slots)):
        for block, found in zip(served, serve(table, rows[:, rows.shape[1] - width :], asking)):
            block[base : base + fetch_slots] = found


def pick_first_kernel(capacity, padded, chips, pick, *refs):
    arrived, refs = refs[:chips], refs[chips:]
    exp_count = (len(refs) - 3) // 2
    grads, refs = refs[:exp_count], refs[exp_count:]
    sent_far, grads_far, (sent, sems) = refs[0], refs[1 : exp_count + 1], refs[exp_count + 1 :]
    put_away = [
        pltpu.make_async_copy(block, place, sems.at[exp_count + step])
        for step, (block, place) in enumerate(zip(grads, grads_far))
    ]
    for copy in put_away:
        copy.start()
    rows = jnp.concatenate([block[...] for block in arrived], axis=0)
    by_slot = dot(pick[...], rows).astype(bf16)
    column = lax.axis_index("exp")
    for step in range(exp_count):
        sent[step] = by_slot[step * padded : step * padded + capacity]
        copy = pltpu.make_async_copy(sent.at[step], sent_far.at[jnp.bitwise_xor(column, step)], sems.at[step])
        copy.start()
        put_away.append(copy)
    for copy in put_away:
        copy.wait()


def pick_last_kernel(capacity, padded, chips, pick, *refs):
    arrived, sent = refs[:chips], refs[chips:]
    rows = jnp.concatenate([block[...] for block in arrived], axis=0)
    by_slot = dot(pick[...], rows).astype(bf16)
    for step in range(len(sent)):
        sent[step][...] = by_slot[step * padded : step * padded + capacity]


def fill(tile, blocks, capacity, padded):
    tile[...] = jnp.zeros(tile.shape, tile.dtype)
    for step, block in enumerate(blocks):
        tile[step * padded : step * padded + capacity, :] = block[...]


def partial_kernel(capacity, padded, gate, down, arrived, turned, pre_act, adapted, tile):
    column = lax.axis_index("exp")
    tile[...] = jnp.zeros(tile.shape, tile.dtype)
    for step in range(arrived.shape[0]):
        tile[step * padded : step * padded + capacity, :] = arrived[jnp.bitwise_xor(column, step)]
    width = tile.shape[1]
    pre_act[...] = dot(tile[...], gate[0, :width])
    adapted[...] = dot(tile[...], down[0, :width])
    turned[...] = tile[...].T


def fetch_kernel(*refs):
    count = (len(refs) - 1) // 2
    sems = refs[-1]
    copies = [pltpu.make_async_copy(refs[i], refs[count + i], sems.at[i]) for i in range(count)]
    for copy in copies:
        copy.start()
    for copy in copies:
        copy.wait()


def forward(rows, pre_first, adapted_first, grads, gate, down, up):
    width = gate.shape[1] - rows.shape[1]
    adapted = (adapted_first + dot(rows, down[0, width:])).astype(bf16)
    pre_act = pre_first + dot(rows, gate[0, width:]) + dot(adapted, up[0])
    gate_value = jax.nn.sigmoid(pre_act)
    activated = (pre_act * gate_value).astype(bf16)
    slope = gate_value * (1.0 + pre_act * (1.0 - gate_value))
    grad_pre = (grads.astype(f32) * slope).astype(bf16)
    back = dot(grad_pre, up[0], ((1,), (1,))).astype(bf16)
    return activated, adapted, grad_pre, back


def early_kernel(capacity, padded, steps, pre_first, adapted_first, gate, down, up, *refs):
    blocks, refs = refs[:steps], refs[steps:]
    grads, refs = refs[:steps], refs[steps:]
    activated, refs = refs[:steps], refs[steps:]
    turned, adapted, grad_pre, back, tile, grad_tile = refs
    fill(tile, blocks, capacity, padded)
    fill(grad_tile, grads, capacity, padded)
    count = tile.shape[0]
    rows, adapted[...], grad_pre[...], back[...] = forward(
        tile[...], pre_first[:count], adapted_first[:count], grad_tile[...], gate, down, up
    )
    for step in range(steps):
        activated[step][...] = rows[step * padded : step * padded + capacity]
    turned[...] = tile[...].T


def late_kernel(
    capacity,
    padded,
    steps,
    turned_first,
    turned_early,
    adapted_early,
    grad_early,
    back_early,
    pre_first,
    adapted_first,
    gate,
    down,
    up,
    *refs,
):
    blocks, refs = refs[:steps], refs[steps:]
    grads, refs = refs[:steps], refs[steps:]
    activated, refs = refs[:steps], refs[steps:]
    keep, give, tile, grad_tile, down_term, up_term = refs
    fill(tile, blocks, capacity, padded)
    fill(grad_tile, grads, capacity, padded)
    count = pre_first.shape[0] - tile.shape[0]
    rows, adapted, grad_pre, back = forward(
        tile[...], pre_first[count:], adapted_first[count:], grad_tile[...], gate, down, up
    )
    for step in range(steps):
        activated[step][...] = rows[step * padded : step * padded + capacity]
    width = turned_first.shape[0]
    down_term[:width] = dot(turned_first[...], jnp.concatenate([back_early[...], back], axis=0))
    down_term[width:] = dot(turned_early[...], back_early[...]) + dot(tile[...], back, ((0,), (0,)))
    owners, up_rows, hidden_units = up_term.shape
    part = dot(
        jnp.concatenate([adapted_early[...], adapted], axis=0),
        jnp.concatenate([grad_early[...], grad_pre], axis=0),
        ((0,), (0,)),
    )
    for owner in range(owners):
        up_term[owner] = part[owner * up_rows : (owner + 1) * up_rows]

    pairs, _, lanes = keep.shape
    down_rows = down_term.shape[0] // owners
    replica = lax.axis_index("rep")
    for chip in range(pairs):
        for flip, target in ((0, keep), (1, give)):
            owner = jnp.bitwise_xor(replica, 2 * chip + flip)
            mine = down_term[pl.ds(pl.multiple_of(owner * down_rows, 8), down_rows)]
            target[chip, :down_rows] = mine.astype(target.dtype)
            mine = up_term[owner].astype(target.dtype)
            for part in range(hidden_units // lanes):
                base = down_rows + part * up_rows
                target[chip, base : base + up_rows] = mine[:, part * lanes : (part + 1) * lanes]


def end_kernel(capacity, padded, chips, home, weight, *refs):
    *refs, down_grad, up_grad, out, tile = refs
    blocks, terms = refs[:-chips], refs[-chips:]
    total = terms[0][...]
    for term in terms[1:]:
        total = total + term[...].astype(f32)
    down_rows = down_grad.shape[1]
    up_rows, hidden_units = up_grad.shape[1:]
    lanes = total.shape[1]
    down_grad[0] = total[:down_rows]
    for part in range(hidden_units // lanes):
        base = down_rows + part * up_rows
        up_grad[0, :, part * lanes : (part + 1) * lanes] = total[base : base + up_rows]
    fill(tile, blocks, capacity, padded)
    out[...] = (upright(weight[...]) * dot(home[...], tile[...])).astype(bf16)


def body(
    replay_buffer_rows,
    shard_request_index,
    replica_fetch_count,
    routes,
    router_route_weight,
    output_gradient,
    frozen_gate_weight,
    adapter_down_weight,
    adapter_up_weight,
):
    rep_count = lax.axis_size("rep")
    exp_count = lax.axis_size("exp")
    pairs = rep_count // 2
    token_count = routes.shape[0]
    shard_rows, model_width = replay_buffer_rows.shape
    fetch_slots = shard_request_index.shape[2]
    hidden_units = frozen_gate_weight.shape[2]
    rank_width = adapter_down_weight.shape[2]
    capacity = 7 * token_count // (4 * exp_count)
    padded = -(-capacity // 16) * 16
    slots = exp_count * padded
    fetched_rows = rep_count * fetch_slots
    first_width = model_width // 128 * FIRST_PART // PARTS * 128
    last_width = model_width - first_width

    routes_row = routes.reshape(1, token_count)
    weight_row = router_route_weight.reshape(1, token_count)

    pair_rows = swap_core(replay_buffer_rows, rep_count)
    pair_table = swap_core(shard_request_index, rep_count)
    operands = [shard_request_index, replay_buffer_rows, routes_row, weight_row, output_gradient]
    far = pl.BlockSpec(memory_space=pltpu.HBM)
    near = pl.BlockSpec(memory_space=pltpu.VMEM)
    served, *grads = pl.pallas_call(
        functools.partial(begin_kernel, capacity, padded),
        out_shape=[shape((pairs, fetch_slots, first_width), bf16)]
        + [shape((capacity, hidden_units), bf16)] * exp_count,
        in_specs=[far] * len(operands),
        out_specs=[near] * (1 + exp_count),
        scratch_shapes=[
            pltpu.VMEM(shard_request_index.shape, i32),
            pltpu.VMEM((shard_rows, first_width), bf16),
            pltpu.VMEM(routes_row.shape, i32),
            pltpu.VMEM(weight_row.shape, f32),
            pltpu.VMEM(output_gradient.shape, bf16),
            pltpu.SemaphoreType.DMA((5,)),
        ],
        compiler_params=pltpu.CompilerParams(vmem_limit_bytes=16 * 1024 * 1024),
        name="begin",
    )(*[pltpu.with_memory_space_constraint(array, pltpu.HBM) for array in operands])
    *grads, pair_table, pair_rows = lax.optimization_barrier((*grads, pair_table, pair_rows))
    served = call(
        serve_first_kernel,
        [shape((2 * fetch_slots, first_width), bf16)] * pairs,
        [pair_table, pair_rows, served],
        flops=2 * fetched_rows * shard_rows * first_width,
        name="serve_first",
    )
    *served, routes_row, pair_rows = lax.optimization_barrier((*served, routes_row, pair_rows))
    arrived = [swap_chip(block, step, rep_count) for step, block in enumerate(served)]
    grads = swap_all(grads, exp_count)
    pick, home = call(
        functools.partial(prepare_kernel, fetch_slots, capacity, padded, exp_count),
        [shape((slots, fetched_rows), bf16), shape((token_count, slots), bf16)],
        [replica_fetch_count, routes_row],
        counts=replica_fetch_count,
        stored=[1],
        flops=2 * token_count * slots * fetched_rows,
        name="prepare",
    )
    sent, *grads = pl.pallas_call(
        functools.partial(pick_first_kernel, capacity, padded, pairs),
        out_shape=[pltpu.HBM((exp_count, capacity, first_width), bf16)]
        + [pltpu.HBM((capacity, hidden_units), bf16)] * exp_count,
        in_specs=[near] * (1 + pairs + exp_count),
        out_specs=[far] * (1 + exp_count),
        scratch_shapes=[
            pltpu.VMEM((exp_count, capacity, first_width), bf16),
            pltpu.SemaphoreType.DMA((2 * exp_count,)),
        ],
        compiler_params=pltpu.CompilerParams(vmem_limit_bytes=16 * 1024 * 1024),
        name="pick_first",
    )(pick, *arrived, *grads[exp_count // 2 :], *grads[: exp_count // 2])
    grads = [*grads[exp_count // 2 :], *grads[: exp_count // 2]]

    pair_rows, sent = lax.optimization_barrier((pair_rows, sent))
    first_blocks = lax.all_to_all(sent, "exp", 0, 0, tiled=True)
    served = call(
        serve_last_kernel,
        [shape((2 * fetch_slots, last_width), bf16)] * pairs,
        [shard_request_index, replay_buffer_rows, pair_table, pair_rows],
        far=[shard_request_index, pair_table],
        flops=2 * fetched_rows * shard_rows * last_width,
        name="serve_last",
    )
    arrived = [swap_chip(block, step, rep_count) for step, block in enumerate(served)]
    first_sent, *sent = call(
        functools.partial(pick_last_kernel, capacity, padded, pairs),
        [shape((capacity, last_width), bf16)] * exp_count,
        [pick, *arrived],
        flops=2 * slots * fetched_rows * last_width,
        name="pick_last",
    )
    weights = [frozen_gate_weight, adapter_down_weight, adapter_up_weight]
    first_sent, *weights = lax.optimization_barrier((first_sent, *weights))
    weights = pl.pallas_call(
        fetch_kernel,
        out_shape=[pltpu.VMEM(array.shape, array.dtype) for array in weights],
        in_specs=[far] * len(weights),
        out_specs=[near] * len(weights),
        scratch_shapes=[pltpu.SemaphoreType.DMA((len(weights),))],
        compiler_params=pltpu.CompilerParams(vmem_limit_bytes=16 * 1024 * 1024),
        name="fetch",
    )(*[pltpu.with_memory_space_constraint(array, pltpu.HBM) for array in weights])
    weights = [pltpu.with_memory_space_constraint(array, pltpu.VMEM) for array in weights]
    last_blocks = swap_all([first_sent, *sent], exp_count)

    turned, pre_first, adapted_first = call(
        functools.partial(partial_kernel, capacity, padded),
        [shape((first_width, slots), bf16), shape((slots, hidden_units), f32), shape((slots, rank_width), f32)],
        [*weights[:2], first_blocks],
        resident=weights,
        scratch=[pltpu.VMEM((slots, first_width), bf16)],
        flops=2 * slots * first_width * (hidden_units + rank_width),
        name="partial",
    )

    term_rows = (model_width + rank_width * hidden_units // rank_width) // rep_count
    steps = exp_count // 2
    count = steps * padded
    *activated, turned_early, adapted_early, grad_early, back_early = call(
        functools.partial(early_kernel, capacity, padded, steps),
        [shape((capacity, hidden_units), bf16)] * steps
        + [
            shape((last_width, count), bf16),
            shape((count, rank_width), bf16),
            shape((count, hidden_units), bf16),
            shape((count, rank_width), bf16),
        ],
        [pre_first, adapted_first, *weights, *last_blocks[:steps], *grads[:steps]],
        resident=weights,
        scratch=[pltpu.VMEM((count, last_width), bf16), pltpu.VMEM((count, hidden_units), bf16)],
        flops=2 * count * last_width * (hidden_units + rank_width),
        name="early",
    )
    count = slots - count
    *late, keep, give = call(
        functools.partial(late_kernel, capacity, padded, exp_count - steps),
        [shape((capacity, hidden_units), bf16)] * (exp_count - steps)
        + [shape((pairs, term_rows, rank_width), kind) for kind in (f32, bf16)],
        [
            turned,
            turned_early,
            adapted_early,
            grad_early,
            back_early,
            pre_first,
            adapted_first,
            *weights,
            *last_blocks[steps:],
            *grads[steps:],
        ],
        resident=weights,
        scratch=[
            pltpu.VMEM((count, last_width), bf16),
            pltpu.VMEM((count, hidden_units), bf16),
            pltpu.VMEM((model_width, rank_width), f32),
            pltpu.VMEM((rep_count, rank_width // rep_count, hidden_units), f32),
        ],
        flops=2 * count * last_width * (hidden_units + rank_width) + 4 * slots * model_width * rank_width,
        name="late",
    )
    activated += late

    pair_terms = swap_core(give, rep_count)
    terms = keep + pair_terms.astype(f32)
    sent_terms = terms[1:].astype(bf16)
    came = [swap_chip(sent_terms[step - 1], step, rep_count) for step in range(1, pairs)]
    results = swap_all(activated, exp_count)

    down_grad, up_grad, out_rows = call(
        functools.partial(end_kernel, capacity, padded, pairs),
        [
            shape((1, model_width // rep_count, rank_width), f32),
            shape((1, rank_width // rep_count, hidden_units), f32),
            shape((token_count, hidden_units), bf16),
        ],
        [home, weight_row, *results, terms[0], *came[::-1]],
        scratch=[pltpu.VMEM((slots, hidden_units), bf16)],
        flops=2 * token_count * slots * hidden_units,
        name="end",
    )
    return (out_rows, down_grad, up_grad)


def solution(mesh):
    placed = (
        P(("rep", "exp"), None),
        P(("rep", "exp"), None, None),
        P(("rep", "exp"), None),
        P(("rep", "exp"), None),
        P(("rep", "exp"), None),
        P(("rep", "exp"), None),
        P("exp", None, None),
        P("exp", None, None),
        P("exp", None, None),
    )
    return jax.shard_map(
        body,
        mesh=mesh,
        in_specs=placed,
        out_specs=(P(("rep", "exp"), None), P("exp", "rep", None), P("exp", "rep", None)),
        check_vma=False,
    )
```

```python
import functools

import jax
import jax.numpy as jnp
from jax import lax
from jax.experimental import pallas as pl
from jax.experimental.pallas import tpu as pltpu
from jax.sharding import PartitionSpec as P

FIRST_PART = 17
PARTS = 28
bf16 = jnp.bfloat16
f32 = jnp.float32
i32 = jnp.int32


def dot(a, b, contract=((1,), (0,))):
    return lax.dot_general(a, b, (contract, ((), ())), preferred_element_type=f32)


def call(kernel, out_shape, operands, counts=None, resident=(), far=(), stored=(), scratch=(), flops=0, vmem=16, name=None):
    first_out = len(operands)
    away = [number for number, array in enumerate(operands) if any(array is other for other in far)]
    moved = [*away, *(first_out + number for number in stored)]
    arrays = [*operands, *out_shape]

    def moving(*refs):
        inner = list(refs)
        copies = {}
        if moved:
            *inner, sems = inner
            near = inner[len(inner) - len(moved) :]
            inner = inner[: len(inner) - len(moved)]
            for place, number in enumerate(moved):
                ends = (inner[number], near[place]) if number < first_out else (near[place], inner[number])
                copies[number] = pltpu.make_async_copy(*ends, sems.at[place])
                inner[number] = near[place]
        for number in away:
            copies[number].start()
        for number in away:
            copies[number].wait()
        kernel(*inner)
        for number in moved[len(away) :]:
            copies[number].start()
        for number in moved[len(away) :]:
            copies[number].wait()

    def space(number):
        array = arrays[number]
        zeros = (0,) * len(array.shape)
        if number in moved:
            return pl.BlockSpec(memory_space=pltpu.HBM)
        if any(array is other for other in resident):
            return pl.BlockSpec(memory_space=pltpu.VMEM)
        if array is counts:
            return pl.BlockSpec(memory_space=pltpu.SMEM)
        return pl.BlockSpec(array.shape, lambda i: zeros)

    near = [pltpu.VMEM(arrays[number].shape, arrays[number].dtype) for number in moved]
    operands = [
        pltpu.with_memory_space_constraint(array, pltpu.HBM) if number in away else array
        for number, array in enumerate(operands)
    ]
    return pl.pallas_call(
        moving,
        out_shape=[
            pltpu.HBM(out.shape, out.dtype) if number in stored else out for number, out in enumerate(out_shape)
        ],
        grid=(1,),
        in_specs=[space(number) for number in range(first_out)],
        out_specs=[space(first_out + number) for number in range(len(out_shape))],
        scratch_shapes=[*scratch, *near] + ([pltpu.SemaphoreType.DMA((len(moved),))] if moved else []),
        cost_estimate=pl.CostEstimate(flops=flops, bytes_accessed=flops // 300, transcendentals=0),
        compiler_params=pltpu.CompilerParams(vmem_limit_bytes=vmem * 1024 * 1024),
        name=name,
    )(*operands)


def shape(dims, kind):
    return jax.ShapeDtypeStruct(dims, kind)


def swap_exp(block, step, exp_count):
    if step == 0:
        return block
    return lax.ppermute(block, "exp", [(i, i ^ step) for i in range(exp_count)])


def swap_all(blocks, exp_count):
    came = list(blocks)
    for step in [*range(exp_count // 2, exp_count), *range(1, exp_count // 2)]:
        came[step] = swap_exp(blocks[step], step, exp_count)
    return came


def swap_core(block, rep_count):
    return lax.ppermute(block, "rep", [(i, i ^ 1) for i in range(rep_count)])


def swap_chip(block, step, rep_count):
    if step == 0:
        return block
    return lax.ppermute(block, "rep", [(i, i ^ (2 * step)) for i in range(rep_count)])


def upright(row):
    count = row.shape[1]
    same = lax.broadcasted_iota(i32, (count, count), 0) == lax.broadcasted_iota(i32, (count, count), 1)
    return jnp.sum(jnp.where(same, row, jnp.zeros_like(row)), axis=1, keepdims=True)


def one_hot(spots):
    return spots.astype(f32).astype(bf16)


def slot_spots(capacity, padded, exp_count, routes):
    tokens = routes.shape[1]
    block = jnp.bitwise_xor(upright(routes[...]), lax.axis_index("exp"))
    chosen = block == lax.broadcasted_iota(i32, (tokens, exp_count), 1)
    above = lax.broadcasted_iota(i32, (tokens, tokens), 1) < lax.broadcasted_iota(i32, (tokens, tokens), 0)
    ranks = dot(one_hot(above), one_hot(chosen))
    rank = jnp.sum(jnp.where(chosen, ranks, 0.0), axis=1, keepdims=True).astype(i32)
    target = block * padded + rank
    return one_hot(target == lax.broadcasted_iota(i32, (tokens, exp_count * padded), 1))


def prepare_kernel(fetch_slots, capacity, padded, exp_count, counts, routes, pick, home):
    tokens = routes.shape[1]
    rep_count = counts.shape[1]
    replica = lax.axis_index("rep")
    position = lax.broadcasted_iota(i32, (tokens, 1), 0)
    source = jnp.zeros((tokens, 1), i32)
    start = jnp.zeros((tokens, 1), i32)
    end = jnp.int32(0)
    for shard in range(rep_count):
        end = end + counts[0, shard]
        passed = position >= end
        source = source + passed.astype(i32)
        start = jnp.where(passed, end, start)
    home_of = slot_spots(capacity, padded, exp_count, routes)
    home[...] = home_of

    places = lax.broadcasted_iota(i32, (tokens, rep_count * fetch_slots), 1)
    place = jnp.bitwise_xor(source, replica) * fetch_slots + position - start
    pick[...] = dot(home_of, one_hot(place == places), ((0,), (0,))).astype(bf16)


def part_of(chunk, width):
    return slice(chunk * width, (chunk + 1) * width)


def serve(table, rows, asking):
    fetch_slots = table.shape[2]
    asked = jnp.concatenate([table[0, pl.ds(replica, 1), :] for replica in asking], axis=1)
    chosen = asked == lax.broadcasted_iota(i32, (rows.shape[0], asked.shape[1]), 0)
    found = dot(one_hot(chosen), rows, ((0,), (0,))).astype(bf16)
    return [found[number * fetch_slots : (number + 1) * fetch_slots] for number in range(len(asking))]


def asking_chips(pairs):
    return [jnp.bitwise_xor(lax.axis_index("rep"), 2 * step) for step in range(pairs)]


def begin_kernel(capacity, padded, table_far, rows_far, routes_far, weight_far, grads_far, *refs):
    served, *sent = refs[:-6]
    table, rows, routes, weight, grads, sems = refs[-6:]
    width = rows.shape[1]
    fetches = [
        pltpu.make_async_copy(far, near, sems.at[number])
        for number, (far, near) in enumerate(
            (
                (routes_far, routes),
                (weight_far, weight),
                (grads_far, grads),
                (table_far, table),
                (rows_far.at[:, :width], rows),
            )
        )
    ]
    for copy in fetches:
        copy.start()
    for copy in fetches[:3]:
        copy.wait()
    home = slot_spots(capacity, padded, len(sent), routes)
    scaled = (upright(weight[...]) * grads[...].astype(f32)).astype(bf16)
    by_slot = dot(home, scaled, ((0,), (0,))).astype(bf16)
    for step in range(len(sent)):
        sent[step][...] = by_slot[step * padded : step * padded + capacity]
    for copy in fetches[3:]:
        copy.wait()
    for step, found in enumerate(serve(table, rows[...], asking_chips(served.shape[0]))):
        served[step] = found


def serve_first_kernel(table, rows, own, *served):
    fetch_slots = own.shape[1]
    width = own.shape[2]
    for step, found in enumerate(serve(table, rows[:, :width], asking_chips(len(served)))):
        served[step][:fetch_slots] = own[step]
        served[step][fetch_slots:] = found


def serve_last_kernel(own_table, own_rows, pair_table, pair_rows, *served):
    fetch_slots = own_table.shape[2]
    width = served[0].shape[1]
    asking = asking_chips(len(served))
    for table, rows, base in ((own_table, own_rows, 0), (pair_table, pair_rows, fetch_slots)):
        for block, found in zip(served, serve(table, rows[:, rows.shape[1] - width :], asking)):
            block[base : base + fetch_slots] = found


def pick_first_kernel(capacity, padded, chips, pick, *refs):
    arrived, refs = refs[:chips], refs[chips:]
    *refs, sems = refs
    kept = sems.shape[0]
    grads, sent, grads_far = refs[:kept], refs[kept : len(refs) - kept], refs[len(refs) - kept :]
    exp_count = len(sent)
    put_away = [
        pltpu.make_async_copy(block, place, sems.at[step]) for step, (block, place) in enumerate(zip(grads, grads_far))
    ]
    for copy in put_away:
        copy.start()
    rows = jnp.concatenate([block[...] for block in arrived], axis=0)
    by_slot = dot(pick[...], rows).astype(bf16)
    for step in range(exp_count):
        sent[step][...] = by_slot[step * padded : step * padded + capacity]
    for copy in put_away:
        copy.wait()


def pick_last_kernel(capacity, padded, chips, pick, *refs):
    arrived, sent = refs[:chips], refs[chips:]
    rows = jnp.concatenate([block[...] for block in arrived], axis=0)
    by_slot = dot(pick[...], rows).astype(bf16)
    for step in range(len(sent)):
        sent[step][...] = by_slot[step * padded : step * padded + capacity]


def fill(tile, blocks, capacity, padded):
    tile[...] = jnp.zeros(tile.shape, tile.dtype)
    for step, block in enumerate(blocks):
        tile[step * padded : step * padded + capacity, :] = block[...]


def partial_kernel(capacity, padded, gate, down, *refs):
    *blocks, turned, pre_act, adapted, tile = refs
    half = len(blocks) // 2
    fill(tile, [*blocks[half:], *blocks[:half]], capacity, padded)
    width = tile.shape[1]
    pre_act[...] = dot(tile[...], gate[0, :width])
    adapted[...] = dot(tile[...], down[0, :width])
    turned[...] = tile[...].T


def fetch_kernel(*refs):
    count = (len(refs) - 1) // 2
    sems = refs[-1]
    copies = [pltpu.make_async_copy(refs[i], refs[count + i], sems.at[i]) for i in range(count)]
    for copy in copies:
        copy.start()
    for copy in copies:
        copy.wait()


def forward(rows, pre_first, adapted_first, grads, gate, down, up):
    width = gate.shape[1] - rows.shape[1]
    adapted = (adapted_first + dot(rows, down[0, width:])).astype(bf16)
    pre_act = pre_first + dot(rows, gate[0, width:]) + dot(adapted, up[0])
    gate_value = jax.nn.sigmoid(pre_act)
    activated = (pre_act * gate_value).astype(bf16)
    slope = gate_value * (1.0 + pre_act * (1.0 - gate_value))
    grad_pre = (grads.astype(f32) * slope).astype(bf16)
    back = dot(grad_pre, up[0], ((1,), (1,))).astype(bf16)
    return activated, adapted, grad_pre, back


def early_kernel(capacity, padded, steps, pre_first, adapted_first, gate, down, up, *refs):
    blocks, refs = refs[:steps], refs[steps:]
    grads, refs = refs[:steps], refs[steps:]
    activated, refs = refs[:steps], refs[steps:]
    turned, adapted, grad_pre, back, tile, grad_tile = refs
    fill(tile, blocks, capacity, padded)
    fill(grad_tile, grads, capacity, padded)
    count = tile.shape[0]
    rows, adapted[...], grad_pre[...], back[...] = forward(
        tile[...], pre_first[:count], adapted_first[:count], grad_tile[...], gate, down, up
    )
    for step in range(steps):
        activated[step][...] = rows[step * padded : step * padded + capacity]
    turned[...] = tile[...].T


def late_kernel(
    capacity,
    padded,
    steps,
    turned_first,
    turned_early,
    adapted_early,
    grad_early,
    back_early,
    pre_first,
    adapted_first,
    gate,
    down,
    up,
    *refs,
):
    blocks, refs = refs[:steps], refs[steps:]
    grads, refs = refs[:steps], refs[steps:]
    activated, refs = refs[:steps], refs[steps:]
    keep, give, tile, grad_tile, down_term, up_term = refs
    fill(tile, blocks, capacity, padded)
    fill(grad_tile, grads, capacity, padded)
    count = pre_first.shape[0] - tile.shape[0]
    rows, adapted, grad_pre, back = forward(
        tile[...], pre_first[count:], adapted_first[count:], grad_tile[...], gate, down, up
    )
    for step in range(steps):
        activated[step][...] = rows[step * padded : step * padded + capacity]
    width = turned_first.shape[0]
    down_term[:width] = dot(turned_first[...], jnp.concatenate([back_early[...], back], axis=0))
    down_term[width:] = dot(turned_early[...], back_early[...]) + dot(tile[...], back, ((0,), (0,)))
    owners, up_rows, hidden_units = up_term.shape
    part = dot(
        jnp.concatenate([adapted_early[...], adapted], axis=0),
        jnp.concatenate([grad_early[...], grad_pre], axis=0),
        ((0,), (0,)),
    )
    for owner in range(owners):
        up_term[owner] = part[owner * up_rows : (owner + 1) * up_rows]

    pairs, _, lanes = keep.shape
    down_rows = down_term.shape[0] // owners
    replica = lax.axis_index("rep")
    for chip in range(pairs):
        for flip, target in ((0, keep), (1, give)):
            owner = jnp.bitwise_xor(replica, 2 * chip + flip)
            mine = down_term[pl.ds(pl.multiple_of(owner * down_rows, 8), down_rows)]
            target[chip, :down_rows] = mine.astype(target.dtype)
            mine = up_term[owner].astype(target.dtype)
            for part in range(hidden_units // lanes):
                base = down_rows + part * up_rows
                target[chip, base : base + up_rows] = mine[:, part * lanes : (part + 1) * lanes]


def end_kernel(capacity, padded, chips, home, weight, *refs):
    *refs, down_grad, up_grad, out, tile = refs
    blocks, terms = refs[:-chips], refs[-chips:]
    total = terms[0][...]
    for term in terms[1:]:
        total = total + term[...].astype(f32)
    down_rows = down_grad.shape[1]
    up_rows, hidden_units = up_grad.shape[1:]
    lanes = total.shape[1]
    down_grad[0] = total[:down_rows]
    for part in range(hidden_units // lanes):
        base = down_rows + part * up_rows
        up_grad[0, :, part * lanes : (part + 1) * lanes] = total[base : base + up_rows]
    fill(tile, blocks, capacity, padded)
    out[...] = (upright(weight[...]) * dot(home[...], tile[...])).astype(bf16)


def body(
    replay_buffer_rows,
    shard_request_index,
    replica_fetch_count,
    routes,
    router_route_weight,
    output_gradient,
    frozen_gate_weight,
    adapter_down_weight,
    adapter_up_weight,
):
    rep_count = lax.axis_size("rep")
    exp_count = lax.axis_size("exp")
    pairs = rep_count // 2
    token_count = routes.shape[0]
    shard_rows, model_width = replay_buffer_rows.shape
    fetch_slots = shard_request_index.shape[2]
    hidden_units = frozen_gate_weight.shape[2]
    rank_width = adapter_down_weight.shape[2]
    capacity = 7 * token_count // (4 * exp_count)
    padded = -(-capacity // 16) * 16
    slots = exp_count * padded
    fetched_rows = rep_count * fetch_slots
    first_width = model_width // 128 * FIRST_PART // PARTS * 128
    last_width = model_width - first_width

    routes_row = routes.reshape(1, token_count)
    weight_row = router_route_weight.reshape(1, token_count)

    pair_rows = swap_core(replay_buffer_rows, rep_count)
    pair_table = swap_core(shard_request_index, rep_count)
    operands = [shard_request_index, replay_buffer_rows, routes_row, weight_row, output_gradient]
    far = pl.BlockSpec(memory_space=pltpu.HBM)
    near = pl.BlockSpec(memory_space=pltpu.VMEM)
    served, *grads = pl.pallas_call(
        functools.partial(begin_kernel, capacity, padded),
        out_shape=[shape((pairs, fetch_slots, first_width), bf16)]
        + [shape((capacity, hidden_units), bf16)] * exp_count,
        in_specs=[far] * len(operands),
        out_specs=[near] * (1 + exp_count),
        scratch_shapes=[
            pltpu.VMEM(shard_request_index.shape, i32),
            pltpu.VMEM((shard_rows, first_width), bf16),
            pltpu.VMEM(routes_row.shape, i32),
            pltpu.VMEM(weight_row.shape, f32),
            pltpu.VMEM(output_gradient.shape, bf16),
            pltpu.SemaphoreType.DMA((5,)),
        ],
        compiler_params=pltpu.CompilerParams(vmem_limit_bytes=16 * 1024 * 1024),
        name="begin",
    )(*[pltpu.with_memory_space_constraint(array, pltpu.HBM) for array in operands])
    *grads, pair_table, pair_rows = lax.optimization_barrier((*grads, pair_table, pair_rows))
    served = call(
        serve_first_kernel,
        [shape((2 * fetch_slots, first_width), bf16)] * pairs,
        [pair_table, pair_rows, served],
        flops=2 * fetched_rows * shard_rows * first_width,
        name="serve_first",
    )
    *served, routes_row, pair_rows = lax.optimization_barrier((*served, routes_row, pair_rows))
    arrived = [swap_chip(block, step, rep_count) for step, block in enumerate(served)]
    grads = swap_all(grads, exp_count)
    pick, home = call(
        functools.partial(prepare_kernel, fetch_slots, capacity, padded, exp_count),
        [shape((slots, fetched_rows), bf16), shape((token_count, slots), bf16)],
        [replica_fetch_count, routes_row],
        counts=replica_fetch_count,
        stored=[1],
        flops=2 * token_count * slots * fetched_rows,
        name="prepare",
    )
    half = exp_count // 2
    kept = [*grads[half:], grads[0]]
    pair_rows, pick = lax.optimization_barrier((pair_rows, pick))
    served_last = call(
        serve_last_kernel,
        [shape((2 * fetch_slots, last_width), bf16)] * pairs,
        [shard_request_index, replay_buffer_rows, pair_table, pair_rows],
        far=[shard_request_index, pair_table],
        flops=2 * fetched_rows * shard_rows * last_width,
        name="serve_last",
    )
    blocks = pl.pallas_call(
        functools.partial(pick_first_kernel, capacity, padded, pairs),
        out_shape=[shape((capacity, first_width), bf16)] * exp_count
        + [pltpu.HBM((capacity, hidden_units), bf16)] * len(kept),
        in_specs=[near] * (1 + pairs + len(kept)),
        out_specs=[near] * exp_count + [far] * len(kept),
        scratch_shapes=[pltpu.SemaphoreType.DMA((len(kept),))],
        compiler_params=pltpu.CompilerParams(vmem_limit_bytes=16 * 1024 * 1024),
        name="pick_first",
    )(pick, *arrived, *kept)
    sent, kept = blocks[:exp_count], blocks[exp_count:]
    grads = [kept[half], *grads[1:half], *kept[:half]]

    joined = lax.optimization_barrier((*served_last, *sent))
    served, sent = joined[:pairs], joined[pairs:]
    first_blocks = swap_all(sent, exp_count)
    arrived = [swap_chip(block, step, rep_count) for step, block in enumerate(served)]
    first_sent, *sent = call(
        functools.partial(pick_last_kernel, capacity, padded, pairs),
        [shape((capacity, last_width), bf16)] * exp_count,
        [pick, *arrived],
        flops=2 * slots * fetched_rows * last_width,
        name="pick_last",
    )
    weights = [frozen_gate_weight, adapter_down_weight, adapter_up_weight]
    first_sent, *weights = lax.optimization_barrier((first_sent, *weights))
    weights = pl.pallas_call(
        fetch_kernel,
        out_shape=[pltpu.VMEM(array.shape, array.dtype) for array in weights],
        in_specs=[far] * len(weights),
        out_specs=[near] * len(weights),
        scratch_shapes=[pltpu.SemaphoreType.DMA((len(weights),))],
        compiler_params=pltpu.CompilerParams(vmem_limit_bytes=16 * 1024 * 1024),
        name="fetch",
    )(*[pltpu.with_memory_space_constraint(array, pltpu.HBM) for array in weights])
    weights = [pltpu.with_memory_space_constraint(array, pltpu.VMEM) for array in weights]
    last_blocks = swap_all([first_sent, *sent], exp_count)

    turned, pre_first, adapted_first = call(
        functools.partial(partial_kernel, capacity, padded),
        [shape((first_width, slots), bf16), shape((slots, hidden_units), f32), shape((slots, rank_width), f32)],
        [*weights[:2], *first_blocks[exp_count // 2 :], *first_blocks[: exp_count // 2]],
        resident=weights,
        scratch=[pltpu.VMEM((slots, first_width), bf16)],
        flops=2 * slots * first_width * (hidden_units + rank_width),
        name="partial",
    )

    term_rows = (model_width + rank_width * hidden_units // rank_width) // rep_count
    steps = exp_count // 2
    count = steps * padded
    *activated, turned_early, adapted_early, grad_early, back_early = call(
        functools.partial(early_kernel, capacity, padded, steps),
        [shape((capacity, hidden_units), bf16)] * steps
        + [
            shape((last_width, count), bf16),
            shape((count, rank_width), bf16),
            shape((count, hidden_units), bf16),
            shape((count, rank_width), bf16),
        ],
        [pre_first, adapted_first, *weights, *last_blocks[:steps], *grads[:steps]],
        resident=weights,
        scratch=[pltpu.VMEM((count, last_width), bf16), pltpu.VMEM((count, hidden_units), bf16)],
        flops=2 * count * last_width * (hidden_units + rank_width),
        name="early",
    )
    count = slots - count
    *late, keep, give = call(
        functools.partial(late_kernel, capacity, padded, exp_count - steps),
        [shape((capacity, hidden_units), bf16)] * (exp_count - steps)
        + [shape((pairs, term_rows, rank_width), kind) for kind in (f32, bf16)],
        [
            turned,
            turned_early,
            adapted_early,
            grad_early,
            back_early,
            pre_first,
            adapted_first,
            *weights,
            *last_blocks[steps:],
            *grads[steps:],
        ],
        resident=weights,
        scratch=[
            pltpu.VMEM((count, last_width), bf16),
            pltpu.VMEM((count, hidden_units), bf16),
            pltpu.VMEM((model_width, rank_width), f32),
            pltpu.VMEM((rep_count, rank_width // rep_count, hidden_units), f32),
        ],
        flops=2 * count * last_width * (hidden_units + rank_width) + 4 * slots * model_width * rank_width,
        name="late",
    )
    activated += late

    pair_terms = swap_core(give, rep_count)
    terms = keep + pair_terms.astype(f32)
    sent_terms = terms[1:].astype(bf16)
    came = [swap_chip(sent_terms[step - 1], step, rep_count) for step in range(1, pairs)]
    results = swap_all(activated, exp_count)

    down_grad, up_grad, out_rows = call(
        functools.partial(end_kernel, capacity, padded, pairs),
        [
            shape((1, model_width // rep_count, rank_width), f32),
            shape((1, rank_width // rep_count, hidden_units), f32),
            shape((token_count, hidden_units), bf16),
        ],
        [home, weight_row, *results, terms[0], *came[::-1]],
        scratch=[pltpu.VMEM((slots, hidden_units), bf16)],
        flops=2 * token_count * slots * hidden_units,
        name="end",
    )
    return (out_rows, down_grad, up_grad)


def solution(mesh):
    placed = (
        P(("rep", "exp"), None),
        P(("rep", "exp"), None, None),
        P(("rep", "exp"), None),
        P(("rep", "exp"), None),
        P(("rep", "exp"), None),
        P(("rep", "exp"), None),
        P("exp", None, None),
        P("exp", None, None),
        P("exp", None, None),
    )
    return jax.shard_map(
        body,
        mesh=mesh,
        in_specs=placed,
        out_specs=(P(("rep", "exp"), None), P("exp", "rep", None), P("exp", "rep", None)),
        check_vma=False,
    )
```

```python
import functools

import jax
import jax.numpy as jnp
from jax import lax
from jax.experimental import pallas as pl
from jax.experimental.pallas import tpu as pltpu
from jax.sharding import PartitionSpec as P

FIRST_PART = 17
PARTS = 28
bf16 = jnp.bfloat16
f32 = jnp.float32
i32 = jnp.int32


def dot(a, b, contract=((1,), (0,))):
    return lax.dot_general(a, b, (contract, ((), ())), preferred_element_type=f32)


def call(kernel, out_shape, operands, counts=None, resident=(), far=(), stored=(), scratch=(), flops=0, vmem=16, name=None):
    first_out = len(operands)
    away = [number for number, array in enumerate(operands) if any(array is other for other in far)]
    moved = [*away, *(first_out + number for number in stored)]
    arrays = [*operands, *out_shape]

    def moving(*refs):
        inner = list(refs)
        copies = {}
        if moved:
            *inner, sems = inner
            near = inner[len(inner) - len(moved) :]
            inner = inner[: len(inner) - len(moved)]
            for place, number in enumerate(moved):
                ends = (inner[number], near[place]) if number < first_out else (near[place], inner[number])
                copies[number] = pltpu.make_async_copy(*ends, sems.at[place])
                inner[number] = near[place]
        for number in away:
            copies[number].start()
        for number in away:
            copies[number].wait()
        kernel(*inner)
        for number in moved[len(away) :]:
            copies[number].start()
        for number in moved[len(away) :]:
            copies[number].wait()

    def space(number):
        array = arrays[number]
        zeros = (0,) * len(array.shape)
        if number in moved:
            return pl.BlockSpec(memory_space=pltpu.HBM)
        if any(array is other for other in resident):
            return pl.BlockSpec(memory_space=pltpu.VMEM)
        if array is counts:
            return pl.BlockSpec(memory_space=pltpu.SMEM)
        return pl.BlockSpec(array.shape, lambda i: zeros)

    near = [pltpu.VMEM(arrays[number].shape, arrays[number].dtype) for number in moved]
    operands = [
        pltpu.with_memory_space_constraint(array, pltpu.HBM) if number in away else array
        for number, array in enumerate(operands)
    ]
    return pl.pallas_call(
        moving,
        out_shape=[
            pltpu.HBM(out.shape, out.dtype) if number in stored else out for number, out in enumerate(out_shape)
        ],
        grid=(1,),
        in_specs=[space(number) for number in range(first_out)],
        out_specs=[space(first_out + number) for number in range(len(out_shape))],
        scratch_shapes=[*scratch, *near] + ([pltpu.SemaphoreType.DMA((len(moved),))] if moved else []),
        cost_estimate=pl.CostEstimate(flops=flops, bytes_accessed=flops // 300, transcendentals=0),
        compiler_params=pltpu.CompilerParams(vmem_limit_bytes=vmem * 1024 * 1024),
        name=name,
    )(*operands)


def shape(dims, kind):
    return jax.ShapeDtypeStruct(dims, kind)


def swap_exp(block, step, exp_count):
    if step == 0:
        return block
    return lax.ppermute(block, "exp", [(i, i ^ step) for i in range(exp_count)])


def swap_all(blocks, exp_count):
    came = list(blocks)
    for step in [*range(exp_count // 2, exp_count), *range(1, exp_count // 2)]:
        came[step] = swap_exp(blocks[step], step, exp_count)
    return came


def swap_core(block, rep_count):
    return lax.ppermute(block, "rep", [(i, i ^ 1) for i in range(rep_count)])


def swap_chip(block, step, rep_count):
    if step == 0:
        return block
    return lax.ppermute(block, "rep", [(i, i ^ (2 * step)) for i in range(rep_count)])


def upright(row):
    count = row.shape[1]
    same = lax.broadcasted_iota(i32, (count, count), 0) == lax.broadcasted_iota(i32, (count, count), 1)
    return jnp.sum(jnp.where(same, row, jnp.zeros_like(row)), axis=1, keepdims=True)


def one_hot(spots):
    return spots.astype(f32).astype(bf16)


def slot_spots(capacity, padded, exp_count, routes):
    tokens = routes.shape[1]
    block = jnp.bitwise_xor(upright(routes[...]), lax.axis_index("exp"))
    chosen = block == lax.broadcasted_iota(i32, (tokens, exp_count), 1)
    above = lax.broadcasted_iota(i32, (tokens, tokens), 1) < lax.broadcasted_iota(i32, (tokens, tokens), 0)
    ranks = dot(one_hot(above), one_hot(chosen))
    rank = jnp.sum(jnp.where(chosen, ranks, 0.0), axis=1, keepdims=True).astype(i32)
    target = block * padded + rank
    return one_hot(target == lax.broadcasted_iota(i32, (tokens, exp_count * padded), 1))


def prepare_kernel(fetch_slots, capacity, padded, exp_count, counts, routes, pick, home):
    tokens = routes.shape[1]
    rep_count = counts.shape[1]
    replica = lax.axis_index("rep")
    position = lax.broadcasted_iota(i32, (tokens, 1), 0)
    source = jnp.zeros((tokens, 1), i32)
    start = jnp.zeros((tokens, 1), i32)
    end = jnp.int32(0)
    for shard in range(rep_count):
        end = end + counts[0, shard]
        passed = position >= end
        source = source + passed.astype(i32)
        start = jnp.where(passed, end, start)
    home_of = slot_spots(capacity, padded, exp_count, routes)
    home[...] = home_of

    places = lax.broadcasted_iota(i32, (tokens, rep_count * fetch_slots), 1)
    place = jnp.bitwise_xor(source, replica) * fetch_slots + position - start
    pick[...] = dot(home_of, one_hot(place == places), ((0,), (0,))).astype(bf16)


def part_of(chunk, width):
    return slice(chunk * width, (chunk + 1) * width)


def serve(table, rows, asking):
    fetch_slots = table.shape[2]
    asked = jnp.concatenate([table[0, pl.ds(replica, 1), :] for replica in asking], axis=1)
    chosen = asked == lax.broadcasted_iota(i32, (rows.shape[0], asked.shape[1]), 0)
    found = dot(one_hot(chosen), rows, ((0,), (0,))).astype(bf16)
    return [found[number * fetch_slots : (number + 1) * fetch_slots] for number in range(len(asking))]


def asking_chips(pairs):
    return [jnp.bitwise_xor(lax.axis_index("rep"), 2 * step) for step in range(pairs)]


def begin_kernel(capacity, padded, table_far, rows_far, routes_far, weight_far, grads_far, *refs):
    served, *sent = refs[:-6]
    table, rows, routes, weight, grads, sems = refs[-6:]
    width = rows.shape[1]
    fetches = [
        pltpu.make_async_copy(far, near, sems.at[number])
        for number, (far, near) in enumerate(
            (
                (routes_far, routes),
                (weight_far, weight),
                (grads_far, grads),
                (table_far, table),
                (rows_far.at[:, :width], rows),
            )
        )
    ]
    for copy in fetches:
        copy.start()
    for copy in fetches[:3]:
        copy.wait()
    home = slot_spots(capacity, padded, len(sent), routes)
    scaled = (upright(weight[...]) * grads[...].astype(f32)).astype(bf16)
    by_slot = dot(home, scaled, ((0,), (0,))).astype(bf16)
    for step in range(len(sent)):
        sent[step][...] = by_slot[step * padded : step * padded + capacity]
    for copy in fetches[3:]:
        copy.wait()
    for step, found in enumerate(serve(table, rows[...], asking_chips(served.shape[0]))):
        served[step] = found


def serve_first_kernel(table, rows, own, *served):
    fetch_slots = own.shape[1]
    width = own.shape[2]
    for step, found in enumerate(serve(table, rows[:, :width], asking_chips(len(served)))):
        served[step][:fetch_slots] = own[step]
        served[step][fetch_slots:] = found


def serve_last_kernel(own_table, own_rows, pair_table, pair_rows, *served):
    fetch_slots = own_table.shape[2]
    width = served[0].shape[1]
    asking = asking_chips(len(served))
    for table, rows, base in ((own_table, own_rows, 0), (pair_table, pair_rows, fetch_slots)):
        for block, found in zip(served, serve(table, rows[:, rows.shape[1] - width :], asking)):
            block[base : base + fetch_slots] = found


def pick_first_kernel(capacity, padded, chips, pick, *refs):
    arrived, refs = refs[:chips], refs[chips:]
    *refs, kept_far, kept, sem = refs
    count = kept.shape[0] // padded
    grads, sent = refs[:count], refs[count:]
    fill(kept, grads, capacity, padded)
    put_away = pltpu.make_async_copy(kept, kept_far, sem)
    put_away.start()
    rows = jnp.concatenate([block[...] for block in arrived], axis=0)
    by_slot = dot(pick[...], rows).astype(bf16)
    for step in range(len(sent)):
        sent[step][...] = by_slot[step * padded : step * padded + capacity]
    put_away.wait()


def pick_last_kernel(capacity, padded, chips, pick, *refs):
    arrived, sent = refs[:chips], refs[chips:]
    rows = jnp.concatenate([block[...] for block in arrived], axis=0)
    by_slot = dot(pick[...], rows).astype(bf16)
    for step in range(len(sent)):
        sent[step][...] = by_slot[step * padded : step * padded + capacity]


def fill(tile, blocks, capacity, padded):
    tile[...] = jnp.zeros(tile.shape, tile.dtype)
    for step, block in enumerate(blocks):
        tile[step * padded : step * padded + capacity, :] = block[...]


def partial_kernel(capacity, padded, gate, down, *refs):
    *blocks, turned, pre_act, adapted, tile = refs
    half = len(blocks) // 2
    fill(tile, [*blocks[half:], *blocks[:half]], capacity, padded)
    width = tile.shape[1]
    pre_act[...] = dot(tile[...], gate[0, :width])
    adapted[...] = dot(tile[...], down[0, :width])
    turned[...] = tile[...].T


def fetch_kernel(*refs):
    count = (len(refs) - 1) // 2
    sems = refs[-1]
    copies = [pltpu.make_async_copy(refs[i], refs[count + i], sems.at[i]) for i in range(count)]
    for copy in copies:
        copy.start()
    for copy in copies:
        copy.wait()


def forward(rows, pre_first, adapted_first, grads, gate, down, up):
    width = gate.shape[1] - rows.shape[1]
    adapted = (adapted_first + dot(rows, down[0, width:])).astype(bf16)
    pre_act = pre_first + dot(rows, gate[0, width:]) + dot(adapted, up[0])
    gate_value = jax.nn.sigmoid(pre_act)
    activated = (pre_act * gate_value).astype(bf16)
    slope = gate_value * (1.0 + pre_act * (1.0 - gate_value))
    grad_pre = (grads.astype(f32) * slope).astype(bf16)
    back = dot(grad_pre, up[0], ((1,), (1,))).astype(bf16)
    return activated, adapted, grad_pre, back


def early_kernel(capacity, padded, steps, pre_first, adapted_first, gate, down, up, *refs):
    blocks, refs = refs[:steps], refs[steps:]
    kept, grads, refs = refs[0], refs[1:steps], refs[steps:]
    activated, refs = refs[:steps], refs[steps:]
    turned, adapted, grad_pre, back, tile, grad_tile = refs
    fill(tile, blocks, capacity, padded)
    grad_tile[:padded] = kept[kept.shape[0] - padded :]
    if grads:
        fill(grad_tile.at[padded:], grads, capacity, padded)
    count = tile.shape[0]
    rows, adapted[...], grad_pre[...], back[...] = forward(
        tile[...], pre_first[:count], adapted_first[:count], grad_tile[...], gate, down, up
    )
    for step in range(steps):
        activated[step][...] = rows[step * padded : step * padded + capacity]
    turned[...] = tile[...].T


def late_kernel(
    capacity,
    padded,
    steps,
    turned_first,
    turned_early,
    adapted_early,
    grad_early,
    back_early,
    pre_first,
    adapted_first,
    gate,
    down,
    up,
    *refs,
):
    blocks, refs = refs[:steps], refs[steps:]
    kept, refs = refs[0], refs[1:]
    activated, refs = refs[:steps], refs[steps:]
    keep, give, tile, down_term, up_term = refs
    fill(tile, blocks, capacity, padded)
    count = pre_first.shape[0] - tile.shape[0]
    rows, adapted, grad_pre, back = forward(
        tile[...], pre_first[count:], adapted_first[count:], kept[: tile.shape[0]], gate, down, up
    )
    for step in range(steps):
        activated[step][...] = rows[step * padded : step * padded + capacity]
    width = turned_first.shape[0]
    down_term[:width] = dot(turned_first[...], jnp.concatenate([back_early[...], back], axis=0))
    down_term[width:] = dot(turned_early[...], back_early[...]) + dot(tile[...], back, ((0,), (0,)))
    owners, up_rows, hidden_units = up_term.shape
    part = dot(
        jnp.concatenate([adapted_early[...], adapted], axis=0),
        jnp.concatenate([grad_early[...], grad_pre], axis=0),
        ((0,), (0,)),
    )
    for owner in range(owners):
        up_term[owner] = part[owner * up_rows : (owner + 1) * up_rows]

    pairs, _, lanes = keep.shape
    down_rows = down_term.shape[0] // owners
    replica = lax.axis_index("rep")
    for chip in range(pairs):
        for flip, target in ((0, keep), (1, give)):
            owner = jnp.bitwise_xor(replica, 2 * chip + flip)
            mine = down_term[pl.ds(pl.multiple_of(owner * down_rows, 8), down_rows)]
            target[chip, :down_rows] = mine.astype(target.dtype)
            mine = up_term[owner].astype(target.dtype)
            for part in range(hidden_units // lanes):
                base = down_rows + part * up_rows
                target[chip, base : base + up_rows] = mine[:, part * lanes : (part + 1) * lanes]


def end_kernel(capacity, padded, chips, home, weight, *refs):
    *refs, down_grad, up_grad, out, tile = refs
    blocks, terms = refs[:-chips], refs[-chips:]
    total = terms[0][...]
    for term in terms[1:]:
        total = total + term[...].astype(f32)
    down_rows = down_grad.shape[1]
    up_rows, hidden_units = up_grad.shape[1:]
    lanes = total.shape[1]
    down_grad[0] = total[:down_rows]
    for part in range(hidden_units // lanes):
        base = down_rows + part * up_rows
        up_grad[0, :, part * lanes : (part + 1) * lanes] = total[base : base + up_rows]
    fill(tile, blocks, capacity, padded)
    out[...] = (upright(weight[...]) * dot(home[...], tile[...])).astype(bf16)


def body(
    replay_buffer_rows,
    shard_request_index,
    replica_fetch_count,
    routes,
    router_route_weight,
    output_gradient,
    frozen_gate_weight,
    adapter_down_weight,
    adapter_up_weight,
):
    rep_count = lax.axis_size("rep")
    exp_count = lax.axis_size("exp")
    pairs = rep_count // 2
    token_count = routes.shape[0]
    shard_rows, model_width = replay_buffer_rows.shape
    fetch_slots = shard_request_index.shape[2]
    hidden_units = frozen_gate_weight.shape[2]
    rank_width = adapter_down_weight.shape[2]
    capacity = 7 * token_count // (4 * exp_count)
    padded = -(-capacity // 16) * 16
    slots = exp_count * padded
    fetched_rows = rep_count * fetch_slots
    first_width = model_width // 128 * FIRST_PART // PARTS * 128
    last_width = model_width - first_width

    routes_row = routes.reshape(1, token_count)
    weight_row = router_route_weight.reshape(1, token_count)

    pair_rows = swap_core(replay_buffer_rows, rep_count)
    pair_table = swap_core(shard_request_index, rep_count)
    operands = [shard_request_index, replay_buffer_rows, routes_row, weight_row, output_gradient]
    far = pl.BlockSpec(memory_space=pltpu.HBM)
    near = pl.BlockSpec(memory_space=pltpu.VMEM)
    served, *grads = pl.pallas_call(
        functools.partial(begin_kernel, capacity, padded),
        out_shape=[shape((pairs, fetch_slots, first_width), bf16)]
        + [shape((capacity, hidden_units), bf16)] * exp_count,
        in_specs=[far] * len(operands),
        out_specs=[near] * (1 + exp_count),
        scratch_shapes=[
            pltpu.VMEM(shard_request_index.shape, i32),
            pltpu.VMEM((shard_rows, first_width), bf16),
            pltpu.VMEM(routes_row.shape, i32),
            pltpu.VMEM(weight_row.shape, f32),
            pltpu.VMEM(output_gradient.shape, bf16),
            pltpu.SemaphoreType.DMA((5,)),
        ],
        compiler_params=pltpu.CompilerParams(vmem_limit_bytes=16 * 1024 * 1024),
        name="begin",
    )(*[pltpu.with_memory_space_constraint(array, pltpu.HBM) for array in operands])
    *grads, pair_table, pair_rows = lax.optimization_barrier((*grads, pair_table, pair_rows))
    served = call(
        serve_first_kernel,
        [shape((2 * fetch_slots, first_width), bf16)] * pairs,
        [pair_table, pair_rows, served],
        flops=2 * fetched_rows * shard_rows * first_width,
        name="serve_first",
    )
    *served, routes_row, pair_rows = lax.optimization_barrier((*served, routes_row, pair_rows))
    arrived = [swap_chip(block, step, rep_count) for step, block in enumerate(served)]
    grads = swap_all(grads, exp_count)
    pick, home = call(
        functools.partial(prepare_kernel, fetch_slots, capacity, padded, exp_count),
        [shape((slots, fetched_rows), bf16), shape((token_count, slots), bf16)],
        [replica_fetch_count, routes_row],
        counts=replica_fetch_count,
        stored=[1],
        flops=2 * token_count * slots * fetched_rows,
        name="prepare",
    )
    half = exp_count // 2
    kept = [*grads[half:], grads[0]]
    pair_rows, pick = lax.optimization_barrier((pair_rows, pick))
    served_last = call(
        serve_last_kernel,
        [shape((2 * fetch_slots, last_width), bf16)] * pairs,
        [shard_request_index, replay_buffer_rows, pair_table, pair_rows],
        far=[shard_request_index, pair_table],
        flops=2 * fetched_rows * shard_rows * last_width,
        name="serve_last",
    )
    blocks = pl.pallas_call(
        functools.partial(pick_first_kernel, capacity, padded, pairs),
        out_shape=[shape((capacity, first_width), bf16)] * exp_count
        + [pltpu.HBM((len(kept) * padded, hidden_units), bf16)],
        in_specs=[near] * (1 + pairs + len(kept)),
        out_specs=[near] * exp_count + [far],
        scratch_shapes=[pltpu.VMEM((len(kept) * padded, hidden_units), bf16), pltpu.SemaphoreType.DMA],
        compiler_params=pltpu.CompilerParams(vmem_limit_bytes=16 * 1024 * 1024),
        name="pick_first",
    )(pick, *arrived, *kept)
    *sent, kept = blocks

    joined = lax.optimization_barrier((*served_last, *sent))
    served, sent = joined[:pairs], joined[pairs:]
    first_blocks = swap_all(sent, exp_count)
    arrived = [swap_chip(block, step, rep_count) for step, block in enumerate(served)]
    first_sent, *sent = call(
        functools.partial(pick_last_kernel, capacity, padded, pairs),
        [shape((capacity, last_width), bf16)] * exp_count,
        [pick, *arrived],
        flops=2 * slots * fetched_rows * last_width,
        name="pick_last",
    )
    weights = [frozen_gate_weight, adapter_down_weight, adapter_up_weight]
    first_sent, *weights = lax.optimization_barrier((first_sent, *weights))
    weights = pl.pallas_call(
        fetch_kernel,
        out_shape=[pltpu.VMEM(array.shape, array.dtype) for array in weights],
        in_specs=[far] * len(weights),
        out_specs=[near] * len(weights),
        scratch_shapes=[pltpu.SemaphoreType.DMA((len(weights),))],
        compiler_params=pltpu.CompilerParams(vmem_limit_bytes=16 * 1024 * 1024),
        name="fetch",
    )(*[pltpu.with_memory_space_constraint(array, pltpu.HBM) for array in weights])
    weights = [pltpu.with_memory_space_constraint(array, pltpu.VMEM) for array in weights]
    last_blocks = swap_all([first_sent, *sent], exp_count)

    turned, pre_first, adapted_first = call(
        functools.partial(partial_kernel, capacity, padded),
        [shape((first_width, slots), bf16), shape((slots, hidden_units), f32), shape((slots, rank_width), f32)],
        [*weights[:2], *first_blocks[exp_count // 2 :], *first_blocks[: exp_count // 2]],
        resident=weights,
        scratch=[pltpu.VMEM((slots, first_width), bf16)],
        flops=2 * slots * first_width * (hidden_units + rank_width),
        name="partial",
    )

    term_rows = (model_width + rank_width * hidden_units // rank_width) // rep_count
    steps = exp_count // 2
    count = steps * padded
    *activated, turned_early, adapted_early, grad_early, back_early = call(
        functools.partial(early_kernel, capacity, padded, steps),
        [shape((capacity, hidden_units), bf16)] * steps
        + [
            shape((last_width, count), bf16),
            shape((count, rank_width), bf16),
            shape((count, hidden_units), bf16),
            shape((count, rank_width), bf16),
        ],
        [pre_first, adapted_first, *weights, *last_blocks[:steps], kept, *grads[1:steps]],
        resident=weights,
        scratch=[pltpu.VMEM((count, last_width), bf16), pltpu.VMEM((count, hidden_units), bf16)],
        flops=2 * count * last_width * (hidden_units + rank_width),
        name="early",
    )
    count = slots - count
    *late, keep, give = call(
        functools.partial(late_kernel, capacity, padded, exp_count - steps),
        [shape((capacity, hidden_units), bf16)] * (exp_count - steps)
        + [shape((pairs, term_rows, rank_width), kind) for kind in (f32, bf16)],
        [
            turned,
            turned_early,
            adapted_early,
            grad_early,
            back_early,
            pre_first,
            adapted_first,
            *weights,
            *last_blocks[steps:],
            kept,
        ],
        resident=weights,
        scratch=[
            pltpu.VMEM((count, last_width), bf16),
            pltpu.VMEM((model_width, rank_width), f32),
            pltpu.VMEM((rep_count, rank_width // rep_count, hidden_units), f32),
        ],
        flops=2 * count * last_width * (hidden_units + rank_width) + 4 * slots * model_width * rank_width,
        name="late",
    )
    activated += late

    pair_terms = swap_core(give, rep_count)
    terms = keep + pair_terms.astype(f32)
    sent_terms = terms[1:].astype(bf16)
    came = [swap_chip(sent_terms[step - 1], step, rep_count) for step in range(1, pairs)]
    results = swap_all(activated, exp_count)

    down_grad, up_grad, out_rows = call(
        functools.partial(end_kernel, capacity, padded, pairs),
        [
            shape((1, model_width // rep_count, rank_width), f32),
            shape((1, rank_width // rep_count, hidden_units), f32),
            shape((token_count, hidden_units), bf16),
        ],
        [home, weight_row, *results, terms[0], *came[::-1]],
        scratch=[pltpu.VMEM((slots, hidden_units), bf16)],
        flops=2 * token_count * slots * hidden_units,
        name="end",
    )
    return (out_rows, down_grad, up_grad)


def solution(mesh):
    placed = (
        P(("rep", "exp"), None),
        P(("rep", "exp"), None, None),
        P(("rep", "exp"), None),
        P(("rep", "exp"), None),
        P(("rep", "exp"), None),
        P(("rep", "exp"), None),
        P("exp", None, None),
        P("exp", None, None),
        P("exp", None, None),
    )
    return jax.shard_map(
        body,
        mesh=mesh,
        in_specs=placed,
        out_specs=(P(("rep", "exp"), None), P("exp", "rep", None), P("exp", "rep", None)),
        check_vma=False,
    )
```

```python
import functools

import jax
import jax.numpy as jnp
from jax import lax
from jax.experimental import pallas as pl
from jax.experimental.pallas import tpu as pltpu
from jax.sharding import PartitionSpec as P

FIRST_PART = 17
PARTS = 28
bf16 = jnp.bfloat16
f32 = jnp.float32
i32 = jnp.int32


def dot(a, b, contract=((1,), (0,))):
    return lax.dot_general(a, b, (contract, ((), ())), preferred_element_type=f32)


def call(kernel, out_shape, operands, counts=None, resident=(), far=(), stored=(), scratch=(), flops=0, vmem=16, name=None):
    first_out = len(operands)
    away = [number for number, array in enumerate(operands) if any(array is other for other in far)]
    moved = [*away, *(first_out + number for number in stored)]
    arrays = [*operands, *out_shape]

    def moving(*refs):
        inner = list(refs)
        copies = {}
        if moved:
            *inner, sems = inner
            near = inner[len(inner) - len(moved) :]
            inner = inner[: len(inner) - len(moved)]
            for place, number in enumerate(moved):
                ends = (inner[number], near[place]) if number < first_out else (near[place], inner[number])
                copies[number] = pltpu.make_async_copy(*ends, sems.at[place])
                inner[number] = near[place]
        for number in away:
            copies[number].start()
        for number in away:
            copies[number].wait()
        kernel(*inner)
        for number in moved[len(away) :]:
            copies[number].start()
        for number in moved[len(away) :]:
            copies[number].wait()

    def space(number):
        array = arrays[number]
        zeros = (0,) * len(array.shape)
        if number in moved:
            return pl.BlockSpec(memory_space=pltpu.HBM)
        if any(array is other for other in resident):
            return pl.BlockSpec(memory_space=pltpu.VMEM)
        if array is counts:
            return pl.BlockSpec(memory_space=pltpu.SMEM)
        return pl.BlockSpec(array.shape, lambda i: zeros)

    near = [pltpu.VMEM(arrays[number].shape, arrays[number].dtype) for number in moved]
    operands = [
        pltpu.with_memory_space_constraint(array, pltpu.HBM) if number in away else array
        for number, array in enumerate(operands)
    ]
    return pl.pallas_call(
        moving,
        out_shape=[
            pltpu.HBM(out.shape, out.dtype) if number in stored else out for number, out in enumerate(out_shape)
        ],
        grid=(1,),
        in_specs=[space(number) for number in range(first_out)],
        out_specs=[space(first_out + number) for number in range(len(out_shape))],
        scratch_shapes=[*scratch, *near] + ([pltpu.SemaphoreType.DMA((len(moved),))] if moved else []),
        cost_estimate=pl.CostEstimate(flops=flops, bytes_accessed=flops // 300, transcendentals=0),
        compiler_params=pltpu.CompilerParams(vmem_limit_bytes=vmem * 1024 * 1024),
        name=name,
    )(*operands)


def shape(dims, kind):
    return jax.ShapeDtypeStruct(dims, kind)


def swap_exp(block, step, exp_count):
    if step == 0:
        return block
    return lax.ppermute(block, "exp", [(i, i ^ step) for i in range(exp_count)])


def swap_all(blocks, exp_count):
    came = list(blocks)
    for step in [*range(exp_count // 2, exp_count), *range(1, exp_count // 2)]:
        came[step] = swap_exp(blocks[step], step, exp_count)
    return came


def swap_core(block, rep_count):
    return lax.ppermute(block, "rep", [(i, i ^ 1) for i in range(rep_count)])


def swap_chip(block, step, rep_count):
    if step == 0:
        return block
    return lax.ppermute(block, "rep", [(i, i ^ (2 * step)) for i in range(rep_count)])


def upright(row):
    count = row.shape[1]
    same = lax.broadcasted_iota(i32, (count, count), 0) == lax.broadcasted_iota(i32, (count, count), 1)
    return jnp.sum(jnp.where(same, row, jnp.zeros_like(row)), axis=1, keepdims=True)


def one_hot(spots):
    return spots.astype(f32).astype(bf16)


def slot_spots(capacity, padded, exp_count, routes):
    tokens = routes.shape[1]
    block = jnp.bitwise_xor(upright(routes[...]), lax.axis_index("exp"))
    chosen = block == lax.broadcasted_iota(i32, (tokens, exp_count), 1)
    above = lax.broadcasted_iota(i32, (tokens, tokens), 1) < lax.broadcasted_iota(i32, (tokens, tokens), 0)
    ranks = dot(one_hot(above), one_hot(chosen))
    rank = jnp.sum(jnp.where(chosen, ranks, 0.0), axis=1, keepdims=True).astype(i32)
    target = block * padded + rank
    return one_hot(target == lax.broadcasted_iota(i32, (tokens, exp_count * padded), 1))


def prepare_kernel(fetch_slots, capacity, padded, exp_count, counts, routes, pick, home):
    tokens = routes.shape[1]
    rep_count = counts.shape[1]
    replica = lax.axis_index("rep")
    position = lax.broadcasted_iota(i32, (tokens, 1), 0)
    source = jnp.zeros((tokens, 1), i32)
    start = jnp.zeros((tokens, 1), i32)
    end = jnp.int32(0)
    for shard in range(rep_count):
        end = end + counts[0, shard]
        passed = position >= end
        source = source + passed.astype(i32)
        start = jnp.where(passed, end, start)
    home_of = slot_spots(capacity, padded, exp_count, routes)
    home[...] = home_of

    places = lax.broadcasted_iota(i32, (tokens, rep_count * fetch_slots), 1)
    place = jnp.bitwise_xor(source, replica) * fetch_slots + position - start
    pick[...] = dot(home_of, one_hot(place == places), ((0,), (0,))).astype(bf16)


def part_of(chunk, width):
    return slice(chunk * width, (chunk + 1) * width)


def asked_spots(table, count, asking):
    asked = jnp.concatenate([table[0, pl.ds(replica, 1), :] for replica in asking], axis=1)
    return one_hot(asked == lax.broadcasted_iota(i32, (count, asked.shape[1]), 0))


def serve(table, rows, asking):
    fetch_slots = table.shape[2]
    asked = jnp.concatenate([table[0, pl.ds(replica, 1), :] for replica in asking], axis=1)
    chosen = asked == lax.broadcasted_iota(i32, (rows.shape[0], asked.shape[1]), 0)
    found = dot(one_hot(chosen), rows, ((0,), (0,))).astype(bf16)
    return [found[number * fetch_slots : (number + 1) * fetch_slots] for number in range(len(asking))]


def asking_chips(pairs):
    return [jnp.bitwise_xor(lax.axis_index("rep"), 2 * step) for step in range(pairs)]


def begin_kernel(capacity, padded, table_far, rows_far, routes_far, weight_far, grads_far, *refs):
    served, *sent = refs[:-6]
    table, rows, routes, weight, grads, sems = refs[-6:]
    width = rows.shape[1]
    ends = (
        (routes_far, routes),
        (weight_far, weight),
        (table_far, table),
        (grads_far, grads),
        (rows_far.at[:, :width], rows),
    )
    fetches = [pltpu.make_async_copy(far, near, sems.at[number]) for number, (far, near) in enumerate(ends)]
    for copy in fetches:
        copy.start()
    fetches[0].wait()
    home = slot_spots(capacity, padded, len(sent), routes)
    fetches[1].wait()
    scale = upright(weight[...])
    fetches[2].wait()
    asked = asked_spots(table, rows.shape[0], asking_chips(served.shape[0]))
    fetches[3].wait()
    by_slot = dot(home, (scale * grads[...].astype(f32)).astype(bf16), ((0,), (0,))).astype(bf16)
    for step in range(len(sent)):
        sent[step][...] = by_slot[step * padded : step * padded + capacity]
    fetches[4].wait()
    found = dot(asked, rows[...], ((0,), (0,))).astype(bf16)
    fetch_slots = served.shape[1]
    for step in range(served.shape[0]):
        served[step] = found[step * fetch_slots : (step + 1) * fetch_slots]


def serve_first_kernel(table, rows, own, *served):
    fetch_slots = own.shape[1]
    width = own.shape[2]
    for step, found in enumerate(serve(table, rows[:, :width], asking_chips(len(served)))):
        served[step][:fetch_slots] = own[step]
        served[step][fetch_slots:] = found


def serve_last_kernel(own_table, own_rows, pair_table, pair_rows, *served):
    fetch_slots = own_table.shape[2]
    width = served[0].shape[1]
    asking = asking_chips(len(served))
    for table, rows, base in ((own_table, own_rows, 0), (pair_table, pair_rows, fetch_slots)):
        for block, found in zip(served, serve(table, rows[:, rows.shape[1] - width :], asking)):
            block[base : base + fetch_slots] = found


def pick_first_kernel(capacity, padded, chips, pick, *refs):
    arrived, refs = refs[:chips], refs[chips:]
    *refs, sems = refs
    kept = sems.shape[0]
    grads, sent, grads_far = refs[:kept], refs[kept : len(refs) - kept], refs[len(refs) - kept :]
    exp_count = len(sent)
    put_away = [
        pltpu.make_async_copy(block, place, sems.at[step]) for step, (block, place) in enumerate(zip(grads, grads_far))
    ]
    for copy in put_away:
        copy.start()
    rows = jnp.concatenate([block[...] for block in arrived], axis=0)
    by_slot = dot(pick[...], rows).astype(bf16)
    for step in range(exp_count):
        sent[step][...] = by_slot[step * padded : step * padded + capacity]
    for copy in put_away:
        copy.wait()


def pick_last_kernel(capacity, padded, chips, pick, *refs):
    arrived, sent = refs[:chips], refs[chips:]
    rows = jnp.concatenate([block[...] for block in arrived], axis=0)
    by_slot = dot(pick[...], rows).astype(bf16)
    for step in range(len(sent)):
        sent[step][...] = by_slot[step * padded : step * padded + capacity]


def fill(tile, blocks, capacity, padded):
    tile[...] = jnp.zeros(tile.shape, tile.dtype)
    for step, block in enumerate(blocks):
        tile[step * padded : step * padded + capacity, :] = block[...]


def partial_kernel(capacity, padded, gate, down, *refs):
    *blocks, turned, pre_act, adapted, tile = refs
    half = len(blocks) // 2
    fill(tile, [*blocks[half:], *blocks[:half]], capacity, padded)
    width = tile.shape[1]
    pre_act[...] = dot(tile[...], gate[0, :width])
    adapted[...] = dot(tile[...], down[0, :width])
    turned[...] = tile[...].T


def fetch_kernel(*refs):
    count = (len(refs) - 1) // 2
    sems = refs[-1]
    copies = [pltpu.make_async_copy(refs[i], refs[count + i], sems.at[i]) for i in range(count)]
    for copy in copies:
        copy.start()
    for copy in copies:
        copy.wait()


def forward(rows, pre_first, adapted_first, grads, gate, down, up):
    width = gate.shape[1] - rows.shape[1]
    adapted = (adapted_first + dot(rows, down[0, width:])).astype(bf16)
    pre_act = pre_first + dot(rows, gate[0, width:]) + dot(adapted, up[0])
    gate_value = jax.nn.sigmoid(pre_act)
    activated = (pre_act * gate_value).astype(bf16)
    slope = gate_value * (1.0 + pre_act * (1.0 - gate_value))
    grad_pre = (grads.astype(f32) * slope).astype(bf16)
    back = dot(grad_pre, up[0], ((1,), (1,))).astype(bf16)
    return activated, adapted, grad_pre, back


def early_kernel(capacity, padded, steps, pre_first, adapted_first, gate, down, up, *refs):
    blocks, refs = refs[:steps], refs[steps:]
    grads, refs = refs[:steps], refs[steps:]
    activated, refs = refs[:steps], refs[steps:]
    turned, adapted, grad_pre, back, tile, grad_tile = refs
    fill(tile, blocks, capacity, padded)
    fill(grad_tile, grads, capacity, padded)
    count = tile.shape[0]
    rows, adapted[...], grad_pre[...], back[...] = forward(
        tile[...], pre_first[:count], adapted_first[:count], grad_tile[...], gate, down, up
    )
    for step in range(steps):
        activated[step][...] = rows[step * padded : step * padded + capacity]
    turned[...] = tile[...].T


def late_kernel(
    capacity,
    padded,
    steps,
    turned_first,
    turned_early,
    adapted_early,
    grad_early,
    back_early,
    pre_first,
    adapted_first,
    gate,
    down,
    up,
    *refs,
):
    blocks, refs = refs[:steps], refs[steps:]
    grads, refs = refs[:steps], refs[steps:]
    activated, refs = refs[:steps], refs[steps:]
    keep, give, tile, grad_tile, turned_last, down_term, up_term = refs
    fill(tile, blocks, capacity, padded)
    fill(grad_tile, grads, capacity, padded)
    count = pre_first.shape[0] - tile.shape[0]
    rows, adapted, grad_pre, back = forward(
        tile[...], pre_first[count:], adapted_first[count:], grad_tile[...], gate, down, up
    )
    for step in range(steps):
        activated[step][...] = rows[step * padded : step * padded + capacity]
    width = turned_first.shape[0]
    turned_last[:, :count] = turned_early[...]
    turned_last[:, count:] = tile[...].T
    back = jnp.concatenate([back_early[...], back], axis=0)
    down_term[:width] = dot(turned_first[...], back)
    down_term[width:] = dot(turned_last[...], back)
    owners, up_rows, hidden_units = up_term.shape
    part = dot(
        jnp.concatenate([adapted_early[...], adapted], axis=0),
        jnp.concatenate([grad_early[...], grad_pre], axis=0),
        ((0,), (0,)),
    )
    for owner in range(owners):
        up_term[owner] = part[owner * up_rows : (owner + 1) * up_rows]

    pairs, _, lanes = keep.shape
    down_rows = down_term.shape[0] // owners
    replica = lax.axis_index("rep")
    for chip in range(pairs):
        for flip, target in ((0, keep), (1, give)):
            owner = jnp.bitwise_xor(replica, 2 * chip + flip)
            mine = down_term[pl.ds(pl.multiple_of(owner * down_rows, 8), down_rows)]
            target[chip, :down_rows] = mine.astype(target.dtype)
            mine = up_term[owner].astype(target.dtype)
            for part in range(hidden_units // lanes):
                base = down_rows + part * up_rows
                target[chip, base : base + up_rows] = mine[:, part * lanes : (part + 1) * lanes]


def end_kernel(capacity, padded, chips, home, weight, *refs):
    *refs, down_grad, up_grad, out, tile = refs
    blocks, terms = refs[:-chips], refs[-chips:]
    total = terms[0][...]
    for term in terms[1:]:
        total = total + term[...].astype(f32)
    down_rows = down_grad.shape[1]
    up_rows, hidden_units = up_grad.shape[1:]
    lanes = total.shape[1]
    down_grad[0] = total[:down_rows]
    for part in range(hidden_units // lanes):
        base = down_rows + part * up_rows
        up_grad[0, :, part * lanes : (part + 1) * lanes] = total[base : base + up_rows]
    fill(tile, blocks, capacity, padded)
    out[...] = (upright(weight[...]) * dot(home[...], tile[...])).astype(bf16)


def body(
    replay_buffer_rows,
    shard_request_index,
    replica_fetch_count,
    routes,
    router_route_weight,
    output_gradient,
    frozen_gate_weight,
    adapter_down_weight,
    adapter_up_weight,
):
    rep_count = lax.axis_size("rep")
    exp_count = lax.axis_size("exp")
    pairs = rep_count // 2
    token_count = routes.shape[0]
    shard_rows, model_width = replay_buffer_rows.shape
    fetch_slots = shard_request_index.shape[2]
    hidden_units = frozen_gate_weight.shape[2]
    rank_width = adapter_down_weight.shape[2]
    capacity = 7 * token_count // (4 * exp_count)
    padded = -(-capacity // 16) * 16
    slots = exp_count * padded
    fetched_rows = rep_count * fetch_slots
    first_width = model_width // 128 * FIRST_PART // PARTS * 128
    last_width = model_width - first_width

    routes_row = routes.reshape(1, token_count)
    weight_row = router_route_weight.reshape(1, token_count)

    pair_rows = swap_core(replay_buffer_rows, rep_count)
    pair_table = swap_core(shard_request_index, rep_count)
    operands = [shard_request_index, replay_buffer_rows, routes_row, weight_row, output_gradient]
    far = pl.BlockSpec(memory_space=pltpu.HBM)
    near = pl.BlockSpec(memory_space=pltpu.VMEM)
    served, *grads = pl.pallas_call(
        functools.partial(begin_kernel, capacity, padded),
        out_shape=[shape((pairs, fetch_slots, first_width), bf16)]
        + [shape((capacity, hidden_units), bf16)] * exp_count,
        in_specs=[far] * len(operands),
        out_specs=[near] * (1 + exp_count),
        scratch_shapes=[
            pltpu.VMEM(shard_request_index.shape, i32),
            pltpu.VMEM((shard_rows, first_width), bf16),
            pltpu.VMEM(routes_row.shape, i32),
            pltpu.VMEM(weight_row.shape, f32),
            pltpu.VMEM(output_gradient.shape, bf16),
            pltpu.SemaphoreType.DMA((5,)),
        ],
        compiler_params=pltpu.CompilerParams(vmem_limit_bytes=16 * 1024 * 1024),
        name="begin",
    )(*[pltpu.with_memory_space_constraint(array, pltpu.HBM) for array in operands])
    *grads, pair_table, pair_rows = lax.optimization_barrier((*grads, pair_table, pair_rows))
    served = call(
        serve_first_kernel,
        [shape((2 * fetch_slots, first_width), bf16)] * pairs,
        [pair_table, pair_rows, served],
        flops=2 * fetched_rows * shard_rows * first_width,
        name="serve_first",
    )
    *served, routes_row, pair_rows = lax.optimization_barrier((*served, routes_row, pair_rows))
    arrived = [swap_chip(block, step, rep_count) for step, block in enumerate(served)]
    grads = swap_all(grads, exp_count)
    pick, home = call(
        functools.partial(prepare_kernel, fetch_slots, capacity, padded, exp_count),
        [shape((slots, fetched_rows), bf16), shape((token_count, slots), bf16)],
        [replica_fetch_count, routes_row],
        counts=replica_fetch_count,
        stored=[1],
        flops=2 * token_count * slots * fetched_rows,
        name="prepare",
    )
    half = exp_count // 2
    kept = [*grads[half:], grads[0]]
    pair_rows, pick = lax.optimization_barrier((pair_rows, pick))
    served_last = call(
        serve_last_kernel,
        [shape((2 * fetch_slots, last_width), bf16)] * pairs,
        [shard_request_index, replay_buffer_rows, pair_table, pair_rows],
        far=[shard_request_index, pair_table],
        flops=2 * fetched_rows * shard_rows * last_width,
        name="serve_last",
    )
    blocks = pl.pallas_call(
        functools.partial(pick_first_kernel, capacity, padded, pairs),
        out_shape=[shape((capacity, first_width), bf16)] * exp_count
        + [pltpu.HBM((capacity, hidden_units), bf16)] * len(kept),
        in_specs=[near] * (1 + pairs + len(kept)),
        out_specs=[near] * exp_count + [far] * len(kept),
        scratch_shapes=[pltpu.SemaphoreType.DMA((len(kept),))],
        compiler_params=pltpu.CompilerParams(vmem_limit_bytes=16 * 1024 * 1024),
        name="pick_first",
    )(pick, *arrived, *kept)
    sent, kept = blocks[:exp_count], blocks[exp_count:]
    grads = [kept[half], *grads[1:half], *kept[:half]]

    joined = lax.optimization_barrier((*served_last, *sent))
    served, sent = joined[:pairs], joined[pairs:]
    first_blocks = swap_all(sent, exp_count)
    arrived = [swap_chip(block, step, rep_count) for step, block in enumerate(served)]
    first_sent, *sent = call(
        functools.partial(pick_last_kernel, capacity, padded, pairs),
        [shape((capacity, last_width), bf16)] * exp_count,
        [pick, *arrived],
        flops=2 * slots * fetched_rows * last_width,
        name="pick_last",
    )
    weights = [frozen_gate_weight, adapter_down_weight, adapter_up_weight]
    first_sent, *weights = lax.optimization_barrier((first_sent, *weights))
    weights = pl.pallas_call(
        fetch_kernel,
        out_shape=[pltpu.VMEM(array.shape, array.dtype) for array in weights],
        in_specs=[far] * len(weights),
        out_specs=[near] * len(weights),
        scratch_shapes=[pltpu.SemaphoreType.DMA((len(weights),))],
        compiler_params=pltpu.CompilerParams(vmem_limit_bytes=16 * 1024 * 1024),
        name="fetch",
    )(*[pltpu.with_memory_space_constraint(array, pltpu.HBM) for array in weights])
    weights = [pltpu.with_memory_space_constraint(array, pltpu.VMEM) for array in weights]
    last_blocks = swap_all([first_sent, *sent], exp_count)

    turned, pre_first, adapted_first = call(
        functools.partial(partial_kernel, capacity, padded),
        [shape((first_width, slots), bf16), shape((slots, hidden_units), f32), shape((slots, rank_width), f32)],
        [*weights[:2], *first_blocks[exp_count // 2 :], *first_blocks[: exp_count // 2]],
        resident=weights,
        scratch=[pltpu.VMEM((slots, first_width), bf16)],
        flops=2 * slots * first_width * (hidden_units + rank_width),
        name="partial",
    )

    term_rows = (model_width + rank_width * hidden_units // rank_width) // rep_count
    steps = exp_count // 2
    count = steps * padded
    *activated, turned_early, adapted_early, grad_early, back_early = call(
        functools.partial(early_kernel, capacity, padded, steps),
        [shape((capacity, hidden_units), bf16)] * steps
        + [
            shape((last_width, count), bf16),
            shape((count, rank_width), bf16),
            shape((count, hidden_units), bf16),
            shape((count, rank_width), bf16),
        ],
        [pre_first, adapted_first, *weights, *last_blocks[:steps], *grads[:steps]],
        resident=weights,
        scratch=[pltpu.VMEM((count, last_width), bf16), pltpu.VMEM((count, hidden_units), bf16)],
        flops=2 * count * last_width * (hidden_units + rank_width),
        name="early",
    )
    count = slots - count
    *late, keep, give = call(
        functools.partial(late_kernel, capacity, padded, exp_count - steps),
        [shape((capacity, hidden_units), bf16)] * (exp_count - steps)
        + [shape((pairs, term_rows, rank_width), kind) for kind in (f32, bf16)],
        [
            turned,
            turned_early,
            adapted_early,
            grad_early,
            back_early,
            pre_first,
            adapted_first,
            *weights,
            *last_blocks[steps:],
            *grads[steps:],
        ],
        resident=weights,
        scratch=[
            pltpu.VMEM((count, last_width), bf16),
            pltpu.VMEM((count, hidden_units), bf16),
            pltpu.VMEM((last_width, slots), bf16),
            pltpu.VMEM((model_width, rank_width), f32),
            pltpu.VMEM((rep_count, rank_width // rep_count, hidden_units), f32),
        ],
        flops=2 * count * last_width * (hidden_units + rank_width) + 4 * slots * model_width * rank_width,
        name="late",
    )
    activated += late

    pair_terms = swap_core(give, rep_count)
    terms = keep + pair_terms.astype(f32)
    sent_terms = terms[1:].astype(bf16)
    came = [swap_chip(sent_terms[step - 1], step, rep_count) for step in range(1, pairs)]
    results = swap_all(activated, exp_count)

    down_grad, up_grad, out_rows = call(
        functools.partial(end_kernel, capacity, padded, pairs),
        [
            shape((1, model_width // rep_count, rank_width), f32),
            shape((1, rank_width // rep_count, hidden_units), f32),
            shape((token_count, hidden_units), bf16),
        ],
        [home, weight_row, *results, terms[0], *came[::-1]],
        scratch=[pltpu.VMEM((slots, hidden_units), bf16)],
        flops=2 * token_count * slots * hidden_units,
        name="end",
    )
    return (out_rows, down_grad, up_grad)


def solution(mesh):
    placed = (
        P(("rep", "exp"), None),
        P(("rep", "exp"), None, None),
        P(("rep", "exp"), None),
        P(("rep", "exp"), None),
        P(("rep", "exp"), None),
        P(("rep", "exp"), None),
        P("exp", None, None),
        P("exp", None, None),
        P("exp", None, None),
    )
    return jax.shard_map(
        body,
        mesh=mesh,
        in_specs=placed,
        out_specs=(P(("rep", "exp"), None), P("exp", "rep", None), P("exp", "rep", None)),
        check_vma=False,
    )
```
